256 devices in a mesh: group: 2 (over core), lat: 4 (over z_lo), lon: 32 (over y, z_hi, x).
Axes of the slice: x: 4, y: 4, z: 8 (z_hi: 2, z_lo: 4; z = z_hi * 4 + z_lo), core: 2. Of those that a mesh axis runs over, the one named last changes fastest.
Arguments:
- states: bfloat16 [2, 64, 1536, 512], P('group', 'lat', 'lon'), may hold values from -6 to 6
- cotangent: bfloat16 [2, 64, 1536, 512], P('group', 'lat', 'lon'), may hold values from -6 to 6
- depth_kernel: float32 [2, 7, 7, 512], P('group'), may hold values from -0.875 to 0.875
- norm_gain: float32 [2, 512], P('group'), may hold values from 0.5 to 1.5
- w_in: bfloat16 [2, 2048, 512], P('group'), may hold values from -0.25 to 0.25
- w_out: bfloat16 [2, 2048, 512], P('group'), may hold values from -0.125 to 0.125
- source_tiles: int32 [2, 4, 32, 4], P('group', 'lat', 'lon'), may hold values from 0 to 127, as said below
- regrid_weights: float32 [2, 64, 1536, 4], P('group', 'lat', 'lon'), may hold values from 0.2 to 1
- land_mask: int32 [64, 1536], P('lat', 'lon'), may hold values 0 or 1
Outputs:
- advanced: bfloat16 [2, 64, 1536, 512], P('group', 'lat', 'lon')
- state_grad: bfloat16 [2, 64, 1536, 512], P('group', 'lat', 'lon')
- grad_w_in: float32 [2, 2048, 512], P('group', ('lat', 'lon'))
- grad_w_out: float32 [2, 2048, 512], P('group', ('lat', 'lon'))
The draws below stay inside these ranges and needn't reach their ends.
Inputs may be any that keep to these rules, and one draw needn't show every extreme that they name: `source_tiles`: entry 0 of each list names the destination tile itself; every entry names a tile whose latitude tile differs from the destination's by at most one and whose longitude tile differs by at most one around the longitude cycle.
All inputs are finite; a program needn't handle non-finite values. No bound on the sum of `land_mask` on one device may be relied on, other than what follows from the above.
Results may differ from the reference program's by a relative error of at most 0.017.
Values may be sent and summed in bfloat16 or wider, within the bound.
No kernel may reach another device: no remote copies, remote signals or barrier semaphores. Data moves between devices by JAX's collectives and lax.ppermute only.
A program may use at most 128 MiB of HBM per device.

```python
import jax
import jax.numpy as jnp
from jax import lax

C = 512
F = 2048
Q = 8
KS = 7
K = 4
CLAT = 16
CLON = 48
NLAT = 64
NLON = 1536
N_LAT = 4
N_LON = 32


def draw_source_tiles(key, part):
    key = jax.random.fold_in(key, 11)
    lat_key, lon_key = jax.random.split(key)
    lat_ids = jnp.arange(N_LAT, dtype=jnp.int32)[None, :, None, None]
    lon_ids = jnp.arange(N_LON, dtype=jnp.int32)[None, None, :, None]
    lat_step = jax.random.randint(lat_key, (2, N_LAT, N_LON, K), -1, 2, dtype=jnp.int32)
    lon_step = jax.random.randint(lon_key, (2, N_LAT, N_LON, K), -1, 2, dtype=jnp.int32)
    leading = (jnp.arange(K, dtype=jnp.int32) == 0)[None, None, None, :]
    lat_step = jnp.where(leading, 0, lat_step)
    lon_step = jnp.where(leading, 0, lon_step)
    src_lat = jnp.clip(lat_ids + lat_step, 0, N_LAT - 1)
    src_lon = (lon_ids + lon_step + N_LON) % N_LON
    return (src_lat * N_LON + src_lon).astype(jnp.int32)


def with_ends(result, key, least, top_value):
    extent = result.shape
    spot = [jax.random.randint(jax.random.fold_in(key, axis), (), 0, extent[axis]) for axis in range(len(extent))]
    result = result.at[tuple(spot)].set(least)
    longest = extent.index(max(extent))
    spot[longest] = (spot[longest] + 1) % extent[longest]
    return result.at[tuple(spot)].set(top_value)


def level_of(stream_key, extent, cuts, smallest, top_value):
    level, own = 1.0, jax.random.fold_in(stream_key, 6)
    for position, blocks in cuts:
        heights = jnp.exp(jax.random.uniform(jax.random.fold_in(own, position), (blocks,), jnp.float32, smallest / len(cuts), top_value / len(cuts)))
        level = level * jnp.repeat(heights, extent[position] // blocks).reshape([-1 if axis == position else 1 for axis in range(len(extent))])
    return level


def normal_values(rng, shape, scale, bound, cuts=(), kind=jnp.bfloat16):
    gain = level_of(rng, shape, cuts, -0.22, 0.18) if cuts else 1.0
    drawn = jax.random.normal(rng, shape, jnp.float32) * scale * gain
    return jnp.minimum(jnp.maximum(drawn, -bound), bound).astype(kind)


def setup_inputs(seed: int = 0) -> dict:
    seeds = jax.random.split(jax.random.key(seed), 10)
    return {
        "states": normal_values(seeds[0], (2, NLAT, NLON, C), 1.0, 6.0, ((0, 2), (1, 4), (2, 32))),
        "cotangent": normal_values(seeds[1], (2, NLAT, NLON, C), 1.0, 6.0, ((0, 2), (1, 4), (2, 32))),
        "depth_kernel": normal_values(seeds[2], (2, KS, KS, C), (KS * KS) ** -0.5, 0.875, ((0, 2),), jnp.float32),
        "norm_gain": jnp.clip(1.0 + 0.1 * jax.random.normal(seeds[3], (2, C), jnp.float32), 0.5, 1.5),
        "w_in": normal_values(seeds[4], (2, F, C), C ** -0.5, 0.25, ((0, 2),)),
        "w_out": normal_values(seeds[5], (2, F, C), F ** -0.5, 0.125, ((0, 2),)),
        "source_tiles": draw_source_tiles(jax.random.fold_in(seeds[9], 71), 0),
        "regrid_weights": jnp.clip(0.2 + 0.8 * jax.random.uniform(seeds[7], (2, NLAT, NLON, K), jnp.float32) ** level_of(seeds[7], (2, NLAT, NLON, K), ((0, 2), (1, 4), (2, 32)), -0.2, 0.2), 0.2, 1.0),
        "land_mask": with_ends((jax.random.randint(seeds[8], (NLAT, NLON), 0, 3) < 2).astype(jnp.int32), jax.random.fold_in(seeds[8], 1), 0, 1),
    }


EPS = 1e-06

def import_fields(states, source_tiles, regrid_weights, component):
    partner = states[1 - component, :, :, :Q]
    tile_view = partner.reshape(N_LAT, CLAT, N_LON, CLON, Q).transpose(0, 2, 1, 3, 4).reshape(N_LAT * N_LON, CLAT, CLON, Q)
    listed = source_tiles[component].reshape(N_LAT * N_LON, K).astype(jnp.int32)
    chosen = tile_view[listed]
    weights = regrid_weights[component].reshape(N_LAT, CLAT, N_LON, CLON, K).transpose(0, 2, 1, 3, 4).reshape(N_LAT * N_LON, CLAT, CLON, K)
    running = jnp.zeros((N_LAT * N_LON, CLAT, CLON, Q), jnp.float32)
    for pair_idx in range(K):
        running = running + weights[:, :, :, pair_idx, None] * chosen[:, pair_idx].astype(jnp.float32)
    return running.reshape(N_LAT, N_LON, CLAT, CLON, Q).transpose(0, 2, 1, 3, 4).reshape(NLAT, NLON, Q)

def depthwise(values_in, kernel):
    rim_width = KS // 2
    padded = jnp.pad(values_in, ((rim_width, rim_width), (0, 0), (0, 0)))
    running = jnp.zeros(values_in.shape, jnp.float32)
    for row_off in range(KS):
        row_band = padded[row_off:row_off + NLAT]
        for col_off in range(KS):
            shifted = jnp.roll(row_band, rim_width - col_off, axis=1)
            running = running + kernel[row_off, col_off] * shifted.astype(jnp.float32)
    return running

def depthwise_back(values_in, kernel):
    rim_width = KS // 2
    padded = jnp.pad(values_in, ((rim_width, rim_width), (0, 0), (0, 0)))
    running = jnp.zeros(values_in.shape, jnp.float32)
    for row_off in range(KS):
        row_band = padded[2 * rim_width - row_off:2 * rim_width - row_off + NLAT]
        for col_off in range(KS):
            shifted = jnp.roll(row_band, col_off - rim_width, axis=1)
            running = running + kernel[row_off, col_off] * shifted.astype(jnp.float32)
    return running

def component_step(states, cotangent, depth_kernel, norm_gain, w_in, w_out, source_tiles, regrid_weights, land_mask, component):
    current = states[component]
    upstream = cotangent[component]
    kernel = depth_kernel[component]
    imported = import_fields(states, source_tiles, regrid_weights, component)
    forcing = (current[:, :, Q:2 * Q].astype(jnp.float32) + imported).astype(jnp.bfloat16)
    forced = jnp.concatenate([current[:, :, :Q], forcing, current[:, :, 2 * Q:]], axis=2)
    hidden = depthwise(forced, kernel)
    centre = lax.optimization_barrier(jnp.mean(hidden, axis=-1, keepdims=True))
    variance = lax.optimization_barrier(jnp.mean(jnp.square(hidden - centre), axis=-1, keepdims=True))
    inv_std = lax.rsqrt(variance + EPS)
    normal_hat = (hidden - centre) * inv_std
    normed = (normal_hat * norm_gain[component]).astype(jnp.bfloat16)
    if component == 1:
        ocean_keep = land_mask.astype(jnp.float32)
    else:
        ocean_keep = jnp.ones((NLAT, NLON), jnp.float32)
    block_rows = CLAT * CLON
    count_blocks = NLAT * NLON // block_rows
    pieces = (normed.reshape(count_blocks, block_rows, C), current.reshape(count_blocks, block_rows, C), upstream.reshape(count_blocks, block_rows, C), ocean_keep.reshape(count_blocks, block_rows, 1))
    w_first = w_in[component]
    w_second = w_out[component]

    def mlp_rows(carried, piece_rows):
        grad_first, grad_second = carried
        normed_rows, current_rows, upstream_rows, keep_rows = piece_rows
        pre_act = jnp.dot(normed_rows, w_first.T, preferred_element_type=jnp.float32)
        active, gelu_back = jax.vjp(jax.nn.gelu, pre_act)
        act_bf = active.astype(jnp.bfloat16)
        update = jnp.dot(act_bf, w_second, preferred_element_type=jnp.float32)
        advanced = (current_rows.astype(jnp.float32) + keep_rows * update).astype(jnp.bfloat16)
        d_update = (keep_rows * upstream_rows.astype(jnp.float32)).astype(jnp.bfloat16)
        d_active = jnp.dot(d_update, w_second.T, preferred_element_type=jnp.float32)
        d_pre = gelu_back(d_active)[0].astype(jnp.bfloat16)
        grad_first = grad_first + jnp.dot(d_pre.T, normed_rows, preferred_element_type=jnp.float32)
        grad_second = grad_second + jnp.dot(act_bf.T, d_update, preferred_element_type=jnp.float32)
        d_normed = jnp.dot(d_pre, w_first, preferred_element_type=jnp.float32)
        return ((grad_first, grad_second), (advanced, d_normed))
    start_grads = (jnp.zeros((F, C), jnp.float32), jnp.zeros((F, C), jnp.float32))
    (grad_first, grad_second), (advanced, d_normed) = lax.scan(mlp_rows, start_grads, pieces)
    advanced = advanced.reshape(NLAT, NLON, C)
    d_normed = d_normed.reshape(NLAT, NLON, C)
    scaled = d_normed * norm_gain[component]
    mean_plain = lax.optimization_barrier(jnp.mean(scaled, axis=-1, keepdims=True))
    mean_mixed = lax.optimization_barrier(jnp.mean(scaled * normal_hat, axis=-1, keepdims=True))
    d_hidden = (inv_std * (scaled - mean_plain - normal_hat * mean_mixed)).astype(jnp.bfloat16)
    d_forced = depthwise_back(d_hidden, kernel)
    state_grad = (upstream.astype(jnp.float32) + d_forced).astype(jnp.bfloat16)
    return (advanced, state_grad, grad_first, grad_second)

def reference(states, cotangent, depth_kernel, norm_gain, w_in, w_out, source_tiles, regrid_weights, land_mask):
    results = [component_step(states, cotangent, depth_kernel, norm_gain, w_in, w_out, source_tiles, regrid_weights, land_mask, component) for component in range(2)]
    advanced = jnp.stack([results[0][0], results[1][0]])
    state_grad = jnp.stack([results[0][1], results[1][1]])
    grad_w_in = jnp.stack([results[0][2], results[1][2]])
    grad_w_out = jnp.stack([results[0][3], results[1][3]])
    return (advanced, state_grad, grad_w_in, grad_w_out)
```

```python
import jax
import jax.numpy as jnp
from jax import lax
from jax.sharding import PartitionSpec as P

Q = 8
K = 4


EPS = 1e-06


def from_partner(x, axis, distance):
    return lax.ppermute(x, axis, [(i, i ^ 1 << distance) for i in range(lax.axis_size(axis))])


def extended(block, sides, width):
    for axis, dim in sides:
        count = lax.axis_size(axis)
        forward = [(i, i + 1) for i in range(count - 1)]
        forward.append((count - 1, 0))
        backward = [(target, source) for source, target in forward]
        low = lax.ppermute(
            lax.slice_in_dim(block, block.shape[dim] - width, None, axis=dim), axis, forward
        )
        high = lax.ppermute(lax.slice_in_dim(block, 0, width, axis=dim), axis, backward)
        block = jnp.concatenate([low, block, high], axis=dim)
    return block


def open_rim(padded, rim_width):
    lat_index = lax.axis_index("lat")
    lat_total = lax.axis_size("lat")
    row_ids = jnp.arange(padded.shape[0])
    inside = ((row_ids >= rim_width) | (lat_index > 0)) & (
        (row_ids < padded.shape[0] - rim_width) | (lat_index < lat_total - 1)
    )
    return jnp.where(inside[:, None, None], padded, jnp.zeros_like(padded))


def conv_taps(padded, kernel, lat_cells, lon_cells, flipped):
    side = kernel.shape[0]
    rim_width = side // 2
    running = jnp.zeros((lat_cells, lon_cells, kernel.shape[2]), jnp.float32)
    for row_off in range(side):
        for col_off in range(side):
            if flipped:
                row_at = 2 * rim_width - row_off
                col_at = 2 * rim_width - col_off
            else:
                row_at = row_off
                col_at = col_off
            window = padded[row_at : row_at + lat_cells, col_at : col_at + lon_cells]
            running = running + kernel[row_off, col_off] * window.astype(jnp.float32)
    return running


def ring(axis):
    return [
        [
            (z % 4) * 32 + y * 8 + (z // 4) * 4 + x
            for x, y, z in (
                [(i, a, b) for i in range(4)]
                if axis == "x"
                else [(a, i, b) for i in range(4)]
                if axis == "y"
                else [(a, b % 4, i) for i in range(8)]
            )
        ]
        for a in range(4)
        for b in range(8 if axis != "z" else 4)
    ]


def scatter_sum(parts, axis, place):
    groups = ring(axis)
    count = len(groups[0])
    total = lax.dynamic_index_in_dim(parts, place, 0, keepdims=False).astype(jnp.float32)
    for step in range(1, count):
        pairs = [(g[i], g[(i + step) % count]) for g in groups for i in range(count)]
        piece = lax.dynamic_index_in_dim(parts, (place + step) % count, 0, keepdims=False)
        total = total + lax.ppermute(piece, ("lat", "lon"), pairs).astype(jnp.float32)
    return total


def reduce_grads(grad_first, grad_second):
    lat, lon = lax.axis_index("lat"), lax.axis_index("lon")
    at_x, at_y, at_z = lon % 4, lon // 8, (lon // 4) % 2 * 4 + lat
    width = grad_first.shape[1]
    first = grad_first.astype(jnp.bfloat16).reshape(4, 4, 2, 4, -1, width)
    second = grad_second.astype(jnp.bfloat16).reshape(4, 4, 2, 4, -1, width)
    first = scatter_sum(first.transpose(3, 1, 2, 0, 4, 5), "x", at_x).astype(jnp.bfloat16)
    second = scatter_sum(second.transpose(1, 3, 2, 0, 4, 5), "y", at_y).astype(jnp.bfloat16)
    first = scatter_sum(first, "y", at_y).astype(jnp.bfloat16)
    second = scatter_sum(second, "x", at_x).astype(jnp.bfloat16)
    both = jnp.concatenate([first, second], axis=-1).reshape(8, -1, 2 * width)
    return scatter_sum(both, "z", at_z)


def body(
    states, cotangent, depth_kernel, norm_gain, w_in, w_out, source_tiles, regrid_weights, land_mask
):
    current = states[0]
    upstream = cotangent[0]
    kernel = depth_kernel[0]
    norm_scale = norm_gain[0]
    w_first = w_in[0]
    w_second = w_out[0]
    lat_cells, lon_cells, channels = current.shape
    cell_count = lat_cells * lon_cells
    rim_width = kernel.shape[0] // 2
    export = current[:, :, :Q]
    partner = from_partner(export, "group", 0)
    sources = source_tiles[0, 0, 0]
    beside_all = extended(partner[None, None], (("lat", 0), ("lon", 1)), 1)
    beside_all = beside_all.reshape(9, lat_cells, lon_cells, Q)
    lon_total = lax.axis_size("lon")
    src_lat = sources // lon_total
    src_lon = sources % lon_total
    lat_step = src_lat - lax.axis_index("lat") + 1
    lon_step = (src_lon - lax.axis_index("lon") + 1 + lon_total) % lon_total
    chosen = beside_all[lat_step * 3 + lon_step]
    running = jnp.zeros((lat_cells, lon_cells, Q), jnp.float32)
    for pair_idx in range(K):
        running = running + regrid_weights[0, :, :, pair_idx, None] * chosen[pair_idx].astype(
            jnp.float32
        )
    forcing = (current[:, :, Q : 2 * Q].astype(jnp.float32) + running).astype(jnp.bfloat16)
    forced = jnp.concatenate([current[:, :, :Q], forcing, current[:, :, 2 * Q :]], axis=2)
    padded = extended(forced, (("lat", 0), ("lon", 1)), rim_width)
    hidden = conv_taps(open_rim(padded, rim_width), kernel, lat_cells, lon_cells, False)
    centre = jnp.mean(hidden, axis=-1, keepdims=True)
    variance = jnp.mean(jnp.square(hidden - centre), axis=-1, keepdims=True)
    inv_std = lax.rsqrt(variance + EPS)
    normal_hat = (hidden - centre) * inv_std
    normed = (normal_hat * norm_scale).astype(jnp.bfloat16).reshape(cell_count, channels)
    pre_act = jnp.einsum("pc,fc->pf", normed, w_first, preferred_element_type=jnp.float32)
    active, gelu_back = jax.vjp(jax.nn.gelu, pre_act)
    act_bf = active.astype(jnp.bfloat16)
    update = jnp.einsum("pf,fc->pc", act_bf, w_second, preferred_element_type=jnp.float32)
    group_index = lax.axis_index("group")
    ocean_keep = jnp.where(group_index == 1, land_mask.astype(jnp.float32), 1.0).reshape(
        cell_count, 1
    )
    flat_now = current.reshape(cell_count, channels)
    advanced = (flat_now.astype(jnp.float32) + ocean_keep * update).astype(jnp.bfloat16)
    d_update = (ocean_keep * upstream.reshape(cell_count, channels).astype(jnp.float32)).astype(
        jnp.bfloat16
    )
    d_active = jnp.einsum("pc,fc->pf", d_update, w_second, preferred_element_type=jnp.float32)
    d_pre = gelu_back(d_active)[0].astype(jnp.bfloat16)
    grad_first = jnp.einsum("pf,pc->fc", d_pre, normed, preferred_element_type=jnp.float32)
    grad_second = jnp.einsum("pf,pc->fc", act_bf, d_update, preferred_element_type=jnp.float32)
    summed = reduce_grads(grad_first, grad_second)
    d_normed = jnp.einsum("pf,fc->pc", d_pre, w_first, preferred_element_type=jnp.float32)
    scaled = d_normed.reshape(lat_cells, lon_cells, channels) * norm_scale
    mean_plain = jnp.mean(scaled, axis=-1, keepdims=True)
    mean_mixed = jnp.mean(scaled * normal_hat, axis=-1, keepdims=True)
    d_hidden = (inv_std * (scaled - mean_plain - normal_hat * mean_mixed)).astype(jnp.bfloat16)
    grad_pad = extended(d_hidden, (("lat", 0), ("lon", 1)), rim_width)
    d_forced = conv_taps(open_rim(grad_pad, rim_width), kernel, lat_cells, lon_cells, True)
    state_grad = (upstream.astype(jnp.float32) + d_forced).astype(jnp.bfloat16)
    return (
        advanced.reshape(1, lat_cells, lon_cells, channels),
        state_grad[None],
        summed[:, :channels][None],
        summed[:, channels:][None],
    )


def solution(mesh):
    placed = (
        P("group", "lat", "lon", None),
        P("group", "lat", "lon", None),
        P("group", None, None, None),
        P("group", None),
        P("group", None, None),
        P("group", None, None),
        P("group", "lat", "lon", None),
        P("group", "lat", "lon", None),
        P("lat", "lon"),
    )
    return jax.shard_map(
        body,
        mesh=mesh,
        in_specs=placed,
        out_specs=(
            P("group", "lat", "lon", None),
            P("group", "lat", "lon", None),
            P("group", ("lat", "lon"), None),
            P("group", ("lat", "lon"), None),
        ),
        check_vma=False,
    )
```

```python
import functools

import jax
import jax.numpy as jnp
from jax import lax
from jax.experimental import pallas as pl
from jax.experimental.pallas import tpu as pltpu
from jax.sharding import PartitionSpec as P

Q = 8
EPS = 1e-06
BF = jnp.bfloat16
F32 = jnp.float32
ROWS, COLS, CH, LANES = 16, 48, 512, 128
CELLS = ROWS * COLS
BLOCKS = CH // LANES
RIM = 3
TAPS = 7
LEFT = 8
PAD_ROWS, PAD_COLS = ROWS + 2 * RIM, 64
HALF = 1024
PART = 256
GELU_A = 0.7978845608028654
GELU_B = 0.044715 * GELU_A


def shape(dims, dtype):
    return jax.ShapeDtypeStruct(dims, dtype)


def run(kernel, name, outs, *args, smem=0, scratch=(), flops=0, moved=1 << 20, views=None, room=4):
    views = views or {}
    in_specs = [
        pl.BlockSpec(memory_space=pltpu.SMEM)
        if at < smem
        else views.get(at, pl.BlockSpec(memory_space=pltpu.VMEM))
        for at in range(len(args))
    ]
    return pl.pallas_call(
        kernel,
        out_shape=outs,
        grid=(1,),
        in_specs=in_specs,
        out_specs=[pl.BlockSpec(memory_space=pltpu.VMEM)] * len(outs),
        scratch_shapes=list(scratch),
        compiler_params=pltpu.CompilerParams(vmem_limit_bytes=room << 20),
        cost_estimate=pl.CostEstimate(flops=flops, bytes_accessed=moved, transcendentals=0),
        name=name,
    )(*args)


def lon_is_even():
    return lax.rem(lax.axis_index("lon"), 2) == 0


def cols_into(packed, row, cells, first):
    packed[3 * row : 3 * row + 3, :] = cells[first : first + 3, :]


def by_parity(even, a, b):
    return jnp.where(even, a, b)


def export_kernel(state_ref, taps_ref, out_ref, top_ref, bottom_ref):
    top_ref[...] = state_ref[0:RIM]
    bottom_ref[...] = state_ref[ROWS - RIM :]
    cells = state_ref[:, :, 0:LANES].reshape(CELLS, LANES).astype(F32)
    out_ref[...] = jnp.concatenate(
        [cells[at * LANES : (at + 1) * LANES].T[:Q] for at in range(CELLS // LANES)], axis=0
    ).astype(BF)


def lon_pack_kernel(state_ref, fields_ref, one_ref, two_ref, left, right):
    for row in range(ROWS):
        cols_into(left, row, state_ref[row, 0:16, LANES:].astype(F32), 0)
        cols_into(right, row, state_ref[row, 32:48, LANES:].astype(F32), 13)
    even = lon_is_even()
    one_ref[:, LANES:] = by_parity(even, right[...], left[...]).astype(BF)
    two_ref[:, LANES:] = by_parity(even, left[...], right[...]).astype(BF)
    one_ref[:, :LANES] = fields_ref[...]
    two_ref[:, :LANES] = fields_ref[...]


def sides(one_ref, two_ref):
    even = lon_is_even()
    one, two = one_ref[...].astype(F32), two_ref[...].astype(F32)
    return by_parity(even, two, one), by_parity(even, one, two)


def lat_pack_kernel(fields_ref, one_ref, two_ref, top_ref, bottom_ref, up_ref, down_ref, hold):
    left, right = sides(one_ref, two_ref)
    hold[0:48, 0:128] = fields_ref[...].astype(F32)
    hold[0:48, 128:256] = left[:, :LANES]
    hold[0:48, 256:384] = right[:, :LANES]
    hold[64:80, :] = jnp.zeros((16, 384), F32)
    for out_ref, at in ((up_ref, 0), (down_ref, 39)):
        hold[48:57, :] = left[at : at + 9, LANES:]
        hold[57:66, :] = right[at : at + 9, LANES:]
        out_ref[...] = hold[...].astype(BF)


def import_kernel(
    source_ref, state_ref, weight_ref, fields_ref, one_ref, two_ref, above_ref, below_ref,
    forced_ref, send_one_ref, send_two_ref, tiles, cells, left, right, flat,
):
    lat, lon = lax.axis_index("lat"), lax.axis_index("lon")
    for row in range(ROWS):
        flat[0:4, row * COLS : (row + 1) * COLS] = weight_ref[row]
    places = []
    for pair in range(4):
        source = source_ref[pair]
        lat_step = source // 32 - lat + 1
        lon_step = lax.rem(lax.rem(source, 32) - lon + 33, 32)
        places.append(jnp.clip(lat_step * 3 + lon_step, 0, 8))
    lon_left, lon_right = sides(one_ref, two_ref)
    tiles[3] = lon_left[:, :LANES]
    tiles[4] = fields_ref[...].astype(F32)
    tiles[5] = lon_right[:, :LANES]
    for at, ref in ((0, above_ref), (6, below_ref)):
        tiles[at + 1] = ref[0:48, 0:128].astype(F32)
        tiles[at] = ref[0:48, 128:256].astype(F32)
        tiles[at + 2] = ref[0:48, 256:384].astype(F32)
    state = state_ref[:, :, 0:LANES].reshape(CELLS, LANES).astype(F32)
    for at in range(CELLS // LANES):
        running = jnp.zeros((Q, LANES), F32)
        for pair in range(4):
            weight = flat[pair : pair + 1, at * LANES : (at + 1) * LANES]
            running = running + weight * tiles[places[pair], at * Q : (at + 1) * Q, :]
        wide = jnp.concatenate(
            [jnp.zeros((Q, LANES), F32), running, jnp.zeros((LANES - 2 * Q, LANES), F32)], axis=0
        )
        cells[at * LANES : (at + 1) * LANES, :] = state[at * LANES : (at + 1) * LANES] + wide.T
    forced_ref[...] = cells[...].astype(BF)
    for row in range(ROWS):
        start = row * COLS
        left[3 * row : 3 * row + 3, :] = cells[start : start + 3, :]
        right[3 * row : 3 * row + 3, :] = cells[start + 45 : start + 48, :]
    even = lon_is_even()
    send_one_ref[...] = by_parity(even, right[...], left[...]).astype(BF)
    send_two_ref[...] = by_parity(even, left[...], right[...]).astype(BF)


def rim_pack_kernel(cells_ref, one_ref, two_ref, after_ref, up_ref, down_ref, hold):
    left, right = sides(one_ref, two_ref)
    width = hold.shape[1]
    hold[16:32, :] = jnp.zeros((16, width), F32)
    for out_ref, first, at in ((up_ref, 0, 0), (down_ref, CELLS - 144, 39)):
        out_ref[0:144, :] = cells_ref[first : first + 144, :]
        hold[0:9, :] = left[at : at + 9]
        hold[9:18, :] = right[at : at + 9]
        out_ref[144:176, :] = hold[...].astype(BF)


def spread_taps(spread, kernel_ref, lane_from, blocks, flipped):
    for at in range(blocks):
        for tap in range(TAPS * TAPS):
            from_tap = TAPS * TAPS - 1 - tap if flipped else tap
            spread[at, tap] = jnp.broadcast_to(kernel_ref[pl.ds(BLOCKS * from_tap + lane_from + at, 1), :], (8, LANES))


def fill_rows(pad, at, top, middle, bottom):
    pad[at, 0:RIM, LEFT : LEFT + COLS, :] = top
    pad[at, RIM : RIM + ROWS, LEFT : LEFT + COLS, :] = middle
    pad[at, RIM + ROWS :, LEFT : LEFT + COLS, :] = bottom


def fill_sides(pad, at, left, right, above, below):
    for row in range(PAD_ROWS):
        if row < RIM:
            one = above[3 * row : 3 * row + 3]
            two = above[9 + 3 * row : 12 + 3 * row]
        elif row < RIM + ROWS:
            one = left[3 * (row - RIM) : 3 * (row - RIM) + 3]
            two = right[3 * (row - RIM) : 3 * (row - RIM) + 3]
        else:
            low = row - RIM - ROWS
            one = below[3 * low : 3 * low + 3]
            two = below[9 + 3 * low : 12 + 3 * low]
        pad[at, row, LEFT - RIM : LEFT, :] = one
        pad[at, row, LEFT + COLS : LEFT + COLS + RIM, :] = two


def convolve(pad, spread, at, emit):
    for chunk in range(3):
        sums = {}
        for row in range(PAD_ROWS):
            first = chunk * 16 + LEFT - RIM
            window = [
                pad[at, row, first + shift : first + shift + 16, :].reshape(2, 8, LANES)
                for shift in range(TAPS)
            ]
            for off in range(TAPS):
                out_row = row - off
                if 0 <= out_row < ROWS:
                    part = window[0] * spread[at, off * TAPS][None]
                    for shift in range(1, TAPS):
                        part = part + window[shift] * spread[at, off * TAPS + shift][None]
                    sums[out_row] = part if off == 0 else sums[out_row] + part
            if row >= TAPS - 1:
                out_row = row - (TAPS - 1)
                emit(out_row, chunk * 16, sums.pop(out_row).reshape(16, LANES))


def conv_wide_kernel(
    state_ref, one_ref, two_ref, top_ref, bottom_ref, above_ref, below_ref, kernel_ref,
    upstream_ref, mask_ref, hidden_ref, update_ref, keep_ref, pad, spread,
):
    left, right = sides(one_ref, two_ref)
    above = above_ref[48:80, :].astype(F32)
    below = below_ref[48:80, :].astype(F32)
    spread_taps(spread, kernel_ref, 1, 3, False)
    for at in range(3):
        wide = slice((at + 1) * LANES, (at + 2) * LANES)
        thin = slice(at * LANES, (at + 1) * LANES)
        fill_rows(
            pad, at, top_ref[:, :, wide].astype(F32), state_ref[:, :, wide].astype(F32),
            bottom_ref[:, :, wide].astype(F32),
        )
        fill_sides(pad, at, left[:, wide], right[:, wide], above[:, thin], below[:, thin])

    def one_block(at, carry):
        def emit(row, col, value):
            hidden_ref[at, row, col : col + 16, :] = value

        convolve(pad, spread, at, emit)
        return carry

    lax.fori_loop(0, 3, one_block, 0)
    mask = jnp.where(lax.axis_index("group") == 1, mask_ref[...].astype(F32), 1.0).T
    for row in range(ROWS):
        rows = slice(row * COLS, (row + 1) * COLS)
        keep_ref[rows, :] = jnp.broadcast_to(mask[:, row : row + 1], (COLS, LANES))

    def one_lane_block(at, carry):
        lanes = pl.ds(pl.multiple_of(at * LANES, LANES), LANES)
        update_ref[:, lanes] = (keep_ref[...] * upstream_ref[:, lanes].astype(F32)).astype(BF)
        return carry

    lax.fori_loop(0, BLOCKS, one_lane_block, 0)


def conv_norm_kernel(
    forced_ref, one_ref, two_ref, above_ref, below_ref, kernel_ref, hidden_ref, gain_ref,
    normed_ref, hat_ref, inv_ref, pad, spread, first,
):
    left, right = sides(one_ref, two_ref)
    above, below = above_ref[...].astype(F32), below_ref[...].astype(F32)
    spread_taps(spread, kernel_ref, 0, 1, False)
    fill_rows(
        pad, 0, above[0:144].reshape(RIM, COLS, LANES),
        forced_ref[...].astype(F32).reshape(ROWS, COLS, LANES), below[0:144].reshape(RIM, COLS, LANES),
    )
    fill_sides(pad, 0, left, right, above[144:176], below[144:176])

    def emit(row, col, value):
        first[row, col : col + 16, :] = value

    convolve(pad, spread, 0, emit)

    def one_row(row, carry):
        parts = [first[row]] + [hidden_ref[at, row] for at in range(3)]
        centre = jnp.sum(sum(parts[1:], parts[0]), axis=-1, keepdims=True) * (1.0 / CH)
        parts = [part - centre for part in parts]
        squares = [part * part for part in parts]
        variance = jnp.sum(sum(squares[1:], squares[0]), axis=-1, keepdims=True) * (1.0 / CH)
        inv = lax.rsqrt(variance + EPS)
        inv_ref[row] = jnp.broadcast_to(inv, (COLS, LANES))
        for at in range(BLOCKS):
            lanes = slice(at * LANES, (at + 1) * LANES)
            hat = parts[at] * inv
            hat_ref[row, :, lanes] = hat
            normed_ref[row, :, lanes] = (hat * gain_ref[:, lanes]).astype(BF)
        return carry

    lax.fori_loop(0, ROWS, one_row, 0)


def dot(a, b, left, right):
    return lax.dot_general(a, b, (((left,), (right,)), ((), ())), preferred_element_type=F32)


def along(axis):
    lon = lax.axis_index("lon")
    if axis == "x":
        return lax.rem(lon, 4)
    if axis == "y":
        return lon // 8
    return lax.rem(lon // 4, 2) * 4 + lax.axis_index("lat")


def mlp_kernel(
    normed_ref, update_ref, w_in_ref, w_out_ref,
    grad0_ref, grad1_ref, grad2_ref, grad3_ref, act_ref, pre_ref, w_in_out_ref, w_out_out_ref,
    *, by_x,
):
    normed = normed_ref[...]
    update = update_ref[...]
    for step, grad_ref in enumerate((grad0_ref, grad1_ref, grad2_ref, grad3_ref)):
        chunk = lax.rem(along("x" if by_x else "y") + step, 4)
        first = w_in_ref[0, :, chunk].reshape(PART, CH)
        second = w_out_ref[0, :, chunk].reshape(PART, CH)
        mine = slice(step * PART, (step + 1) * PART)
        w_in_out_ref[mine, :] = first
        w_out_out_ref[mine, :] = second
        value = dot(normed, first, 1, 1)
        square = value * value
        bent = jnp.tanh(value * (GELU_A + GELU_B * square))
        cdf = 0.5 + 0.5 * bent
        act = (value * cdf).astype(BF)
        slope = cdf + (0.5 * value) * (1.0 - bent * bent) * (GELU_A + 3.0 * GELU_B * square)
        pre = (dot(update, second, 1, 1) * slope).astype(BF)
        act_ref[:, mine] = act
        pre_ref[:, mine] = pre
        grad_ref[:, :CH] = dot(pre, normed, 0, 0).astype(BF)
        grad_ref[:, CH:] = dot(act, update, 0, 0).astype(BF)


def finish_kernel(
    act_a_ref, act_b_ref, pre_a_ref, pre_b_ref, w_in_a_ref, w_in_b_ref, w_out_a_ref, w_out_b_ref,
    state_ref, keep_ref, gain_ref, hat_ref, inv_ref,
    advanced_ref, d_hidden_ref, one_ref, two_ref, wide, left, right,
):
    wide[...] = dot(act_a_ref[...], w_out_a_ref[...], 1, 0) + dot(act_b_ref[...], w_out_b_ref[...], 1, 0)
    for at in range(BLOCKS):
        lanes = slice(at * LANES, (at + 1) * LANES)
        advanced_ref[:, lanes] = (state_ref[:, lanes].astype(F32) + keep_ref[...] * wide[:, lanes]).astype(BF)
    wide[...] = dot(pre_a_ref[...], w_in_a_ref[...], 1, 0) + dot(pre_b_ref[...], w_in_b_ref[...], 1, 0)

    def one_row(row, carry):
        rows = pl.ds(pl.multiple_of(row * COLS, COLS), COLS)
        hat = hat_ref[rows, :]
        scaled = wide[rows, :] * gain_ref[...]
        plain = jnp.sum(scaled, axis=-1, keepdims=True) * (1.0 / CH)
        mixed = jnp.sum(scaled * hat, axis=-1, keepdims=True) * (1.0 / CH)
        back = inv_ref[rows, 0:1] * (scaled - plain - hat * mixed)
        wide[rows, :] = back
        d_hidden_ref[rows, :] = back.astype(BF)
        return carry

    lax.fori_loop(0, ROWS, one_row, 0)
    for row in range(ROWS):
        start = row * COLS
        left[3 * row : 3 * row + 3, :] = wide[start : start + 3, :]
        right[3 * row : 3 * row + 3, :] = wide[start + 45 : start + 48, :]
    even = lon_is_even()
    one_ref[...] = by_parity(even, right[...], left[...]).astype(BF)
    two_ref[...] = by_parity(even, left[...], right[...]).astype(BF)


def conv_back_kernel(
    d_hidden_ref, one_ref, two_ref, above_ref, below_ref, kernel_ref, upstream_ref,
    out_ref, pad, spread, held,
):
    left, right = sides(one_ref, two_ref)
    spread_taps(spread, kernel_ref, 0, BLOCKS, True)
    for at in range(BLOCKS):
        lanes = slice(at * LANES, (at + 1) * LANES)
        above, below = above_ref[:, lanes].astype(F32), below_ref[:, lanes].astype(F32)
        fill_rows(
            pad, at, above[0:144].reshape(RIM, COLS, LANES),
            d_hidden_ref[:, lanes].astype(F32).reshape(ROWS, COLS, LANES),
            below[0:144].reshape(RIM, COLS, LANES),
        )
        fill_sides(pad, at, left[:, lanes], right[:, lanes], above[144:176], below[144:176])

    def one_block(at, carry):
        def emit(row, col, value):
            held[at, row, col : col + 16, :] = value

        convolve(pad, spread, at, emit)
        return carry

    lax.fori_loop(0, BLOCKS, one_block, 0)
    for at in range(BLOCKS):
        lanes = slice(at * LANES, (at + 1) * LANES)
        out_ref[:, :, lanes] = (upstream_ref[:, :, lanes].astype(F32) + held[at]).astype(BF)


def sum_refs(refs):
    total = refs[0][...].astype(F32)
    for ref in refs[1:]:
        total = total + ref[...].astype(F32)
    return total


def sum_four_kernel(a, b, c, d, out0, out1, out2, out3, hold, *, by_x):
    hold[...] = sum_refs((a, b, c, d)).astype(BF).reshape(hold.shape)
    for step, out in enumerate((out0, out1, out2, out3)):
        chunk = lax.rem(along("y" if by_x else "x") + step, 4)
        if by_x:
            out[...] = hold[:, chunk].reshape(out.shape)
        else:
            out[...] = hold[:, :, chunk].reshape(out.shape)


def sum_eight_kernel(*refs):
    ins, outs, hold = refs[:8], refs[8:16], refs[16]
    hold[0:4] = sum_refs(ins[:4]).astype(BF).reshape(4, 16, 2 * CH)
    hold[4:8] = sum_refs(ins[4:]).astype(BF).reshape(4, 16, 2 * CH)
    for step, out in enumerate(outs):
        at = lax.rem(along("z") + step, 8)
        out[...] = hold[lax.rem(at, 4) * 2 + at // 4]


def sum_last_kernel(*refs):
    total = sum_refs(refs[:8])
    refs[8][...] = total[:, :CH]
    refs[9][...] = total[:, CH:]


def ring(axis):
    if axis == "x":
        lines = [[(i, a, b) for i in range(4)] for a in range(4) for b in range(8)]
    elif axis == "y":
        lines = [[(a, i, b) for i in range(4)] for a in range(4) for b in range(8)]
    else:
        lines = [[(a, b, i) for i in range(8)] for a in range(4) for b in range(4)]
    return [[(z % 4) * 32 + y * 8 + (z // 4) * 4 + x for x, y, z in line] for line in lines]


def around(pieces, axis):
    groups = ring(axis)
    count = len(groups[0])
    got = [pieces[0]]
    for step in range(1, count):
        pairs = [(g[i], g[(i + step) % count]) for g in groups for i in range(count)]
        got.append(lax.ppermute(pieces[step], ("lat", "lon"), pairs))
    return got


def swap_lon(one, two):
    pairs = [(i, i ^ 1) for i in range(32)]
    other = [(i, (i - 1) % 32 if i % 2 == 0 else (i + 1) % 32) for i in range(32)]
    return lax.ppermute(one, "lon", pairs), lax.ppermute(two, "lon", other)


def swap_lat(up, down):
    above = lax.ppermute(down, "lat", [(i, i + 1) for i in range(3)])
    below = lax.ppermute(up, "lat", [(i + 1, i) for i in range(3)])
    return above, below


def body(
    states, cotangent, depth_kernel, norm_gain, w_in, w_out, source_tiles, regrid_weights, land_mask
):
    vm = pltpu.VMEM
    state = states[0]
    upstream = cotangent[0]
    taps = depth_kernel[0].reshape(TAPS * TAPS * BLOCKS, LANES)
    sources = source_tiles.reshape(4)
    weights = regrid_weights[0].transpose(0, 2, 1)

    mine, top, bottom = run(
        export_kernel, "export", [shape((48, LANES), BF)] + [shape((RIM, COLS, CH), BF)] * 2, state, taps,
        views={1: pl.BlockSpec(memory_space=pl.ANY)},
    )
    fields = lax.ppermute(mine, "group", [(0, 1), (1, 0)])
    top, bottom = swap_lat(top, bottom)
    one, two = run(
        lon_pack_kernel, "lon_pack", [shape((48, CH), BF)] * 2, state, fields,
        scratch=[vm((48, 384), F32)] * 2,
    )
    one, two = swap_lon(one, two)
    up, down = run(
        lat_pack_kernel, "lat_pack", [shape((80, 384), BF)] * 2, fields, one, two, top, bottom,
        scratch=[vm((80, 384), F32)],
    )
    above, below = swap_lat(up, down)
    forced, f_one, f_two = run(
        import_kernel, "import", [shape((CELLS, LANES), BF)] + [shape((48, LANES), BF)] * 2,
        sources, state, weights, fields, one, two, above, below, smem=1,
        scratch=[vm((9, 48, LANES), F32), vm((CELLS, LANES), F32)] + [vm((48, LANES), F32)] * 2
        + [vm((8, CELLS), F32)],
    )
    f_one, f_two = swap_lon(f_one, f_two)
    hidden, update, keep = run(
        conv_wide_kernel, "conv_wide",
        [shape((3, ROWS, COLS, LANES), F32), shape((CELLS, CH), BF), shape((CELLS, LANES), F32)],
        state, one, two, top, bottom, above, below, taps, upstream.reshape(CELLS, CH), land_mask,
        scratch=[vm((3, PAD_ROWS, PAD_COLS, LANES), F32), vm((3, 49, 8, LANES), F32)], moved=8 << 20, room=8,
    )
    f_up, f_down = run(
        rim_pack_kernel, "rim_pack", [shape((176, LANES), BF)] * 2, forced, f_one, f_two, hidden,
        scratch=[vm((32, LANES), F32)], views={3: pl.BlockSpec(memory_space=pl.ANY)},
    )
    f_above, f_below = swap_lat(f_up, f_down)
    normed, hat, inv = run(
        conv_norm_kernel, "conv_norm",
        [shape((ROWS, COLS, CH), BF), shape((ROWS, COLS, CH), F32), shape((ROWS, COLS, LANES), F32)],
        forced, f_one, f_two, f_above, f_below, taps, hidden, norm_gain,
        scratch=[vm((1, PAD_ROWS, PAD_COLS, LANES), F32), vm((1, 49, 8, LANES), F32), vm((ROWS, COLS, LANES), F32)],
        moved=8 << 20, room=6,
    )
    normed = normed.reshape(CELLS, CH)
    hat = hat.reshape(CELLS, CH)
    inv = inv.reshape(CELLS, LANES)

    def half(by_x):
        if by_x:
            dims, block, at = (2, 16, 4, 16, CH), (1, 16, 4, 16, CH), lambda i: (0, 0, 0, 0, 0)
        else:
            dims, block, at = (2, 2, 4, 128, CH), (1, 2, 4, 128, CH), lambda i: (1, 0, 0, 0, 0)
        view = pl.BlockSpec(block, at)
        outs = run(
            functools.partial(mlp_kernel, by_x=by_x), "mlp_x" if by_x else "mlp_y",
            [shape((PART, 2 * CH), BF)] * 4 + [shape((CELLS, HALF), BF)] * 2 + [shape((HALF, CH), BF)] * 2,
            normed, update, w_in[0].reshape(dims), w_out[0].reshape(dims), views={2: view, 3: view}, flops=4 << 30, moved=10 << 20, room=12,
        )
        return outs[:4], outs[4:]

    grads_a, kept_a = half(True)
    grads_a = around(grads_a, "x")
    grads_b, kept_b = half(False)
    grads_b = around(grads_b, "y")
    advanced, d_hidden, d_one, d_two = run(
        finish_kernel, "finish", [shape((CELLS, CH), BF)] * 2 + [shape((48, CH), BF)] * 2,
        kept_a[0], kept_b[0], kept_a[1], kept_b[1], kept_a[2], kept_b[2], kept_a[3], kept_b[3],
        state.reshape(CELLS, CH), keep, norm_gain, hat, inv,
        scratch=[vm((CELLS, CH), F32)] + [vm((48, CH), F32)] * 2, flops=4 << 30, moved=10 << 20, room=12,
    )
    d_one, d_two = swap_lon(d_one, d_two)
    d_up, d_down = run(
        rim_pack_kernel, "rim_pack_back", [shape((176, CH), BF)] * 2, d_hidden, d_one, d_two, d_one,
        scratch=[vm((32, CH), F32)], views={3: pl.BlockSpec(memory_space=pl.ANY)},
    )
    d_above, d_below = swap_lat(d_up, d_down)
    (state_grad,) = run(
        conv_back_kernel, "conv_back", [shape((ROWS, COLS, CH), BF)],
        d_hidden, d_one, d_two, d_above, d_below, taps, upstream,
        scratch=[
            vm((BLOCKS, PAD_ROWS, PAD_COLS, LANES), F32), vm((BLOCKS, 49, 8, LANES), F32),
            vm((BLOCKS, ROWS, COLS, LANES), F32),
        ],
        moved=10 << 20, room=10,
    )
    grads_a = run(
        functools.partial(sum_four_kernel, by_x=True), "sum_x", [shape((64, 2 * CH), BF)] * 4,
        *grads_a, scratch=[vm((2, 4, 32, 2 * CH), BF)],
    )
    grads_a = around(grads_a, "y")
    grads_b = run(
        functools.partial(sum_four_kernel, by_x=False), "sum_y", [shape((64, 2 * CH), BF)] * 4,
        *grads_b, scratch=[vm((2, 2, 4, 16, 2 * CH), BF)],
    )
    grads_b = around(grads_b, "x")
    grads = run(
        sum_eight_kernel, "sum_xy", [shape((16, 2 * CH), BF)] * 8, *grads_a, *grads_b,
        scratch=[vm((8, 16, 2 * CH), BF)],
    )
    grads = around(grads, "z")
    grad_in, grad_out = run(sum_last_kernel, "sum_z", [shape((16, CH), F32)] * 2, *grads)
    return (
        advanced.reshape(1, ROWS, COLS, CH),
        state_grad[None],
        grad_in[None],
        grad_out[None],
    )


def solution(mesh):
    placed = (
        P("group", "lat", "lon", None),
        P("group", "lat", "lon", None),
        P("group", None, None, None),
        P("group", None),
        P("group", None, None),
        P("group", None, None),
        P("group", "lat", "lon", None),
        P("group", "lat", "lon", None),
        P("lat", "lon"),
    )
    return jax.shard_map(
        body,
        mesh=mesh,
        in_specs=placed,
        out_specs=(
            P("group", "lat", "lon", None),
            P("group", "lat", "lon", None),
            P("group", ("lat", "lon"), None),
            P("group", ("lat", "lon"), None),
        ),
        check_vma=False,
    )
```

```python
import functools

import jax
import jax.numpy as jnp
from jax import lax
from jax.experimental import pallas as pl
from jax.experimental.pallas import tpu as pltpu
from jax.sharding import PartitionSpec as P

Q = 8
EPS = 1e-06
BF = jnp.bfloat16
F32 = jnp.float32
ROWS, COLS, CH, LANES = 16, 48, 512, 128
CELLS = ROWS * COLS
BLOCKS = CH // LANES
RIM = 3
TAPS = 7
LEFT = 8
PAD_ROWS, PAD_COLS = ROWS + 2 * RIM, 64
HALF = 1024
PART = 256
GELU_A = 0.7978845608028654
GELU_B = 0.044715 * GELU_A


def shape(dims, dtype):
    return jax.ShapeDtypeStruct(dims, dtype)


def run(kernel, name, outs, *args, smem=0, scratch=(), views=None, room=4, same=None):
    views = views or {}
    in_specs = [
        pl.BlockSpec(memory_space=pltpu.SMEM)
        if at < smem
        else views.get(at, pl.BlockSpec(memory_space=pltpu.VMEM))
        for at in range(len(args))
    ]
    return pl.pallas_call(
        kernel,
        out_shape=outs,
        grid=(1,),
        in_specs=in_specs,
        out_specs=[pl.BlockSpec(memory_space=pltpu.VMEM)] * len(outs),
        scratch_shapes=list(scratch),
        input_output_aliases=same or {},
        compiler_params=pltpu.CompilerParams(vmem_limit_bytes=room << 20),
        cost_estimate=pl.CostEstimate(flops=0, bytes_accessed=1024, transcendentals=0),
        name=name,
    )(*args)


def lon_is_even():
    return lax.rem(lax.axis_index("lon"), 2) == 0


def cols_into(packed, row, cells, first):
    packed[3 * row : 3 * row + 3, :] = cells[first : first + 3, :]


def by_parity(even, a, b):
    return jnp.where(even, a, b)


def export_kernel(state_ref, taps_ref, out_ref):
    cells = state_ref[:, :, 0:LANES].reshape(CELLS, LANES).astype(F32)
    out_ref[...] = jnp.concatenate(
        [cells[at * LANES : (at + 1) * LANES].T[:Q] for at in range(CELLS // LANES)], axis=0
    ).astype(BF)


def lon_pack_kernel(state_ref, fields_ref, one_ref, two_ref, left, right):
    for row in range(ROWS):
        cols_into(left, row, state_ref[row, 0:16, LANES:].astype(F32), 0)
        cols_into(right, row, state_ref[row, 32:48, LANES:].astype(F32), 13)
    even = lon_is_even()
    one_ref[:, LANES:] = by_parity(even, right[...], left[...]).astype(BF)
    two_ref[:, LANES:] = by_parity(even, left[...], right[...]).astype(BF)
    one_ref[:, :LANES] = fields_ref[...]
    two_ref[:, :LANES] = fields_ref[...]


def sides(one_ref, two_ref):
    even = lon_is_even()
    one, two = one_ref[...].astype(F32), two_ref[...].astype(F32)
    return by_parity(even, two, one), by_parity(even, one, two)


def lat_pack_kernel(fields_ref, one_ref, two_ref, state_ref, up_ref, down_ref, hold):
    up_ref[80:224, :] = state_ref[0:RIM, :, LANES:].reshape(144, 384)
    down_ref[80:224, :] = state_ref[ROWS - RIM :, :, LANES:].reshape(144, 384)
    left, right = sides(one_ref, two_ref)
    hold[0:48, 0:128] = fields_ref[...].astype(F32)
    hold[0:48, 128:256] = left[:, :LANES]
    hold[0:48, 256:384] = right[:, :LANES]
    hold[64:80, :] = jnp.zeros((16, 384), F32)
    for out_ref, at in ((up_ref, 0), (down_ref, 39)):
        hold[48:57, :] = left[at : at + 9, LANES:]
        hold[57:66, :] = right[at : at + 9, LANES:]
        out_ref[0:80, :] = hold[...].astype(BF)


def import_kernel(
    source_ref, state_ref, weight_ref, fields_ref, one_ref, two_ref, above_ref, below_ref,
    forced_ref, send_one_ref, send_two_ref, tiles, cells, left, right, flat,
):
    lat, lon = lax.axis_index("lat"), lax.axis_index("lon")
    for row in range(ROWS):
        flat[0:4, row * COLS : (row + 1) * COLS] = weight_ref[row]
    places = []
    for pair in range(4):
        source = source_ref[pair]
        lat_step = source // 32 - lat + 1
        lon_step = lax.rem(lax.rem(source, 32) - lon + 33, 32)
        places.append(jnp.clip(lat_step * 3 + lon_step, 0, 8))
    lon_left, lon_right = sides(one_ref, two_ref)
    tiles[3] = lon_left[:, :LANES]
    tiles[4] = fields_ref[...].astype(F32)
    tiles[5] = lon_right[:, :LANES]
    for at, ref in ((0, above_ref), (6, below_ref)):
        tiles[at + 1] = ref[0:48, 0:128].astype(F32)
        tiles[at] = ref[0:48, 128:256].astype(F32)
        tiles[at + 2] = ref[0:48, 256:384].astype(F32)
    state = state_ref[:, :, 0:LANES].reshape(CELLS, LANES).astype(F32)
    for at in range(CELLS // LANES):
        running = jnp.zeros((Q, LANES), F32)
        for pair in range(4):
            weight = flat[pair : pair + 1, at * LANES : (at + 1) * LANES]
            running = running + weight * tiles[places[pair], at * Q : (at + 1) * Q, :]
        wide = jnp.concatenate(
            [jnp.zeros((Q, LANES), F32), running, jnp.zeros((LANES - 2 * Q, LANES), F32)], axis=0
        )
        cells[at * LANES : (at + 1) * LANES, :] = state[at * LANES : (at + 1) * LANES] + wide.T
    forced_ref[...] = cells[...].astype(BF)
    for row in range(ROWS):
        start = row * COLS
        left[3 * row : 3 * row + 3, :] = cells[start : start + 3, :]
        right[3 * row : 3 * row + 3, :] = cells[start + 45 : start + 48, :]
    even = lon_is_even()
    send_one_ref[...] = by_parity(even, right[...], left[...]).astype(BF)
    send_two_ref[...] = by_parity(even, left[...], right[...]).astype(BF)


def rim_pack_kernel(cells_ref, one_ref, two_ref, after_ref, up_ref, down_ref, hold):
    left, right = sides(one_ref, two_ref)
    width = hold.shape[1]
    hold[16:32, :] = jnp.zeros((16, width), F32)
    for out_ref, first, at in ((up_ref, 0, 0), (down_ref, CELLS - 144, 39)):
        out_ref[0:144, :] = cells_ref[first : first + 144, :]
        hold[0:9, :] = left[at : at + 9]
        hold[9:18, :] = right[at : at + 9]
        out_ref[144:176, :] = hold[...].astype(BF)


def spread_taps(spread, kernel_ref, lane_from, blocks, flipped):
    for at in range(blocks):
        for tap in range(TAPS * TAPS):
            from_tap = TAPS * TAPS - 1 - tap if flipped else tap
            spread[at, tap] = jnp.broadcast_to(kernel_ref[pl.ds(BLOCKS * from_tap + lane_from + at, 1), :], (8, LANES))


def fill_rows(pad, at, top, middle, bottom):
    pad[at, 0:RIM, LEFT : LEFT + COLS, :] = top
    pad[at, RIM : RIM + ROWS, LEFT : LEFT + COLS, :] = middle
    pad[at, RIM + ROWS :, LEFT : LEFT + COLS, :] = bottom


def fill_sides(pad, at, left, right, above, below):
    for row in range(PAD_ROWS):
        if row < RIM:
            one = above[3 * row : 3 * row + 3]
            two = above[9 + 3 * row : 12 + 3 * row]
        elif row < RIM + ROWS:
            one = left[3 * (row - RIM) : 3 * (row - RIM) + 3]
            two = right[3 * (row - RIM) : 3 * (row - RIM) + 3]
        else:
            low = row - RIM - ROWS
            one = below[3 * low : 3 * low + 3]
            two = below[9 + 3 * low : 12 + 3 * low]
        pad[at, row, LEFT - RIM : LEFT, :] = one
        pad[at, row, LEFT + COLS : LEFT + COLS + RIM, :] = two


def convolve(pad, spread, at, emit):
    for chunk in range(3):
        sums = {}
        for row in range(PAD_ROWS):
            first = chunk * 16 + LEFT - RIM
            window = [
                pad[at, row, first + shift : first + shift + 16, :].reshape(2, 8, LANES)
                for shift in range(TAPS)
            ]
            for off in range(TAPS):
                out_row = row - off
                if 0 <= out_row < ROWS:
                    part = window[0] * spread[at, off * TAPS][None]
                    for shift in range(1, TAPS):
                        part = part + window[shift] * spread[at, off * TAPS + shift][None]
                    sums[out_row] = part if off == 0 else sums[out_row] + part
            if row >= TAPS - 1:
                out_row = row - (TAPS - 1)
                emit(out_row, chunk * 16, sums.pop(out_row).reshape(16, LANES))


def conv_wide_kernel(
    state_ref, one_ref, two_ref, above_ref, below_ref, kernel_ref,
    upstream_ref, mask_ref, hidden_ref, update_ref, keep_ref, pad, spread,
):
    left, right = sides(one_ref, two_ref)
    above = above_ref[48:80, :].astype(F32)
    below = below_ref[48:80, :].astype(F32)
    spread_taps(spread, kernel_ref, 1, 3, False)
    for at in range(3):
        wide = slice((at + 1) * LANES, (at + 2) * LANES)
        thin = slice(at * LANES, (at + 1) * LANES)
        fill_rows(
            pad, at, above_ref[80:224, thin].astype(F32).reshape(RIM, COLS, LANES),
            state_ref[:, :, wide].astype(F32), below_ref[80:224, thin].astype(F32).reshape(RIM, COLS, LANES),
        )
        fill_sides(pad, at, left[:, wide], right[:, wide], above[:, thin], below[:, thin])

    def one_block(at, carry):
        def emit(row, col, value):
            hidden_ref[at, row, col : col + 16, :] = value

        convolve(pad, spread, at, emit)
        return carry

    lax.fori_loop(0, 3, one_block, 0)
    mask = jnp.where(lax.axis_index("group") == 1, mask_ref[...].astype(F32), 1.0).T
    for row in range(ROWS):
        rows = slice(row * COLS, (row + 1) * COLS)
        keep_ref[rows, :] = jnp.broadcast_to(mask[:, row : row + 1], (COLS, LANES))

    def one_lane_block(at, carry):
        lanes = pl.ds(pl.multiple_of(at * LANES, LANES), LANES)
        update_ref[:, lanes] = (keep_ref[...] * upstream_ref[:, lanes].astype(F32)).astype(BF)
        return carry

    lax.fori_loop(0, BLOCKS, one_lane_block, 0)


def conv_norm_kernel(
    forced_ref, one_ref, two_ref, above_ref, below_ref, kernel_ref, hidden_ref, gain_ref,
    normed_ref, hat_ref, inv_ref, pad, spread, first,
):
    left, right = sides(one_ref, two_ref)
    above, below = above_ref[...].astype(F32), below_ref[...].astype(F32)
    spread_taps(spread, kernel_ref, 0, 1, False)
    fill_rows(
        pad, 0, above[0:144].reshape(RIM, COLS, LANES),
        forced_ref[...].astype(F32).reshape(ROWS, COLS, LANES), below[0:144].reshape(RIM, COLS, LANES),
    )
    fill_sides(pad, 0, left, right, above[144:176], below[144:176])

    def emit(row, col, value):
        first[row, col : col + 16, :] = value

    convolve(pad, spread, 0, emit)

    def one_row(row, carry):
        parts = [first[row]] + [hidden_ref[at, row] for at in range(3)]
        centre = jnp.sum(sum(parts[1:], parts[0]), axis=-1, keepdims=True) * (1.0 / CH)
        parts = [part - centre for part in parts]
        squares = [part * part for part in parts]
        variance = jnp.sum(sum(squares[1:], squares[0]), axis=-1, keepdims=True) * (1.0 / CH)
        inv = lax.rsqrt(variance + EPS)
        inv_ref[row] = jnp.broadcast_to(inv, (COLS, LANES))
        for at in range(BLOCKS):
            lanes = slice(at * LANES, (at + 1) * LANES)
            hat = parts[at] * inv
            hat_ref[row, :, lanes] = hat
            normed_ref[row, :, lanes] = (hat * gain_ref[:, lanes]).astype(BF)
        return carry

    lax.fori_loop(0, ROWS, one_row, 0)


def dot(a, b, left, right):
    return lax.dot_general(a, b, (((left,), (right,)), ((), ())), preferred_element_type=F32)


def along(axis):
    lon = lax.axis_index("lon")
    if axis == "x":
        return lax.rem(lon, 4)
    if axis == "y":
        return lon // 8
    return lax.rem(lon // 4, 2)


def mlp_kernel(
    normed_ref, update_ref, w_in_ref, w_out_ref,
    grad0_ref, grad1_ref, grad2_ref, grad3_ref, act_ref, pre_ref, w_in_out_ref, w_out_out_ref,
    *, by_x,
):
    normed = normed_ref[...]
    update = update_ref[...]
    for step, grad_ref in enumerate((grad0_ref, grad1_ref, grad2_ref, grad3_ref)):
        chunk = lax.rem(along("x" if by_x else "y") + step, 4)
        first = w_in_ref[0, :, chunk].reshape(PART, CH)
        second = w_out_ref[0, :, chunk].reshape(PART, CH)
        mine = slice(step * PART, (step + 1) * PART)
        w_in_out_ref[mine, :] = first
        w_out_out_ref[mine, :] = second
        value = dot(normed, first, 1, 1)
        square = value * value
        bent = jnp.tanh(value * (GELU_A + GELU_B * square))
        cdf = 0.5 + 0.5 * bent
        act = (value * cdf).astype(BF)
        slope = cdf + (0.5 * value) * (1.0 - bent * bent) * (GELU_A + 3.0 * GELU_B * square)
        pre = (dot(update, second, 1, 1) * slope).astype(BF)
        act_ref[:, mine] = act
        pre_ref[:, mine] = pre
        grad_ref[:, :CH] = dot(pre, normed, 0, 0).astype(BF)
        grad_ref[:, CH:] = dot(act, update, 0, 0).astype(BF)


def advance_kernel(
    act_a_ref, act_b_ref, w_out_a_ref, w_out_b_ref, state_ref, keep_ref, after_ref, advanced_ref, wide
):
    wide[...] = dot(act_a_ref[...], w_out_a_ref[...], 1, 0) + dot(act_b_ref[...], w_out_b_ref[...], 1, 0)
    for at in range(BLOCKS):
        lanes = slice(at * LANES, (at + 1) * LANES)
        advanced_ref[:, lanes] = (state_ref[:, lanes].astype(F32) + keep_ref[...] * wide[:, lanes]).astype(BF)


def finish_kernel(
    pre_a_ref, pre_b_ref, w_in_a_ref, w_in_b_ref, gain_ref, hat_ref, inv_ref, passed_ref,
    d_hidden_ref, one_ref, two_ref, passed_out_ref, wide, left, right,
):
    wide[...] = dot(pre_a_ref[...], w_in_a_ref[...], 1, 0) + dot(pre_b_ref[...], w_in_b_ref[...], 1, 0)

    def one_row(row, carry):
        rows = pl.ds(pl.multiple_of(row * COLS, COLS), COLS)
        hat = hat_ref[rows, :]
        scaled = wide[rows, :] * gain_ref[...]
        plain = jnp.sum(scaled, axis=-1, keepdims=True) * (1.0 / CH)
        mixed = jnp.sum(scaled * hat, axis=-1, keepdims=True) * (1.0 / CH)
        back = inv_ref[rows, 0:1] * (scaled - plain - hat * mixed)
        wide[rows, :] = back
        d_hidden_ref[rows, :] = back.astype(BF)
        return carry

    lax.fori_loop(0, ROWS, one_row, 0)
    for row in range(ROWS):
        start = row * COLS
        left[3 * row : 3 * row + 3, :] = wide[start : start + 3, :]
        right[3 * row : 3 * row + 3, :] = wide[start + 45 : start + 48, :]
    even = lon_is_even()
    one_ref[...] = by_parity(even, right[...], left[...]).astype(BF)
    two_ref[...] = by_parity(even, left[...], right[...]).astype(BF)


def conv_back_kernel(
    d_hidden_ref, one_ref, two_ref, above_ref, below_ref, kernel_ref, upstream_ref, after_ref,
    out_ref, pad, spread, held,
):
    left, right = sides(one_ref, two_ref)
    spread_taps(spread, kernel_ref, 0, BLOCKS, True)
    for at in range(BLOCKS):
        lanes = slice(at * LANES, (at + 1) * LANES)
        above, below = above_ref[:, lanes].astype(F32), below_ref[:, lanes].astype(F32)
        fill_rows(
            pad, at, above[0:144].reshape(RIM, COLS, LANES),
            d_hidden_ref[:, lanes].astype(F32).reshape(ROWS, COLS, LANES),
            below[0:144].reshape(RIM, COLS, LANES),
        )
        fill_sides(pad, at, left[:, lanes], right[:, lanes], above[144:176], below[144:176])

    def one_block(at, carry):
        def emit(row, col, value):
            held[at, row, col : col + 16, :] = value

        convolve(pad, spread, at, emit)
        return carry

    lax.fori_loop(0, BLOCKS, one_block, 0)
    for at in range(BLOCKS):
        lanes = slice(at * LANES, (at + 1) * LANES)
        out_ref[:, :, lanes] = (upstream_ref[:, :, lanes].astype(F32) + held[at]).astype(BF)


def sum_refs(refs):
    total = refs[0][...].astype(F32)
    for ref in refs[1:]:
        total = total + ref[...].astype(F32)
    return total


def sum_four_kernel(a, b, c, d, after, out0, out1, out2, out3, hold, *, by_x):
    hold[...] = sum_refs((a, b, c, d)).astype(BF).reshape(hold.shape)
    for step, out in enumerate((out0, out1, out2, out3)):
        chunk = lax.rem(along("y" if by_x else "x") + step, 4)
        if by_x:
            out[...] = hold[:, chunk].reshape(out.shape)
        else:
            out[...] = hold[:, :, chunk].reshape(out.shape)


def sum_eight_kernel(*refs):
    ins, (mine, other), hold = refs[:8], refs[8:10], refs[10]
    hold[0:2] = sum_refs(ins[:4]).astype(BF).reshape(2, 2, 16, 2 * CH)
    hold[2:4] = sum_refs(ins[4:]).astype(BF).reshape(2, 2, 16, 2 * CH)
    at = along("z_hi")
    mine[...] = hold[:, at].reshape(64, 2 * CH)
    other[...] = hold[:, 1 - at].reshape(64, 2 * CH)


def sum_two_kernel(a, b, after, out0, out1, out2, out3, hold):
    hold[...] = sum_refs((a, b)).astype(BF).reshape(4, 16, 2 * CH)
    for step, out in enumerate((out0, out1, out2, out3)):
        out[...] = hold[lax.rem(lax.axis_index("lat") + step, 4)]


def sum_last_kernel(*refs):
    total = sum_refs(refs[:4])
    refs[4][...] = total[:, :CH]
    refs[5][...] = total[:, CH:]


def ring(axis):
    if axis == "x":
        lines = [[(i, a, b) for i in range(4)] for a in range(4) for b in range(8)]
    elif axis == "y":
        lines = [[(a, i, b) for i in range(4)] for a in range(4) for b in range(8)]
    elif axis == "z_hi":
        lines = [[(a, b, i + 4 * j) for j in range(2)] for a in range(4) for b in range(4) for i in range(4)]
    else:
        lines = [[(a, b, i + 4 * j) for i in range(4)] for a in range(4) for b in range(4) for j in range(2)]
    return [[(z % 4) * 32 + y * 8 + (z // 4) * 4 + x for x, y, z in line] for line in lines]


def send(piece, axis, step):
    groups = ring(axis)
    count = len(groups[0])
    pairs = [(g[i], g[(i + step) % count]) for g in groups for i in range(count)]
    return lax.ppermute(piece, ("lat", "lon"), pairs)


def around(pieces, axis):
    return [pieces[0]] + [send(piece, axis, step) for step, piece in enumerate(pieces) if step]


def swap_lon(one, two):
    pairs = [(i, i ^ 1) for i in range(32)]
    other = [(i, (i - 1) % 32 if i % 2 == 0 else (i + 1) % 32) for i in range(32)]
    two = lax.ppermute(two, "lon", other)
    return lax.ppermute(one, "lon", pairs), two


def swap_lat(up, down):
    above = lax.ppermute(down, "lat", [(i, i + 1) for i in range(3)])
    below = lax.ppermute(up, "lat", [(i + 1, i) for i in range(3)])
    return above, below


def body(
    states, cotangent, depth_kernel, norm_gain, w_in, w_out, source_tiles, regrid_weights, land_mask
):
    vm = pltpu.VMEM
    state = states[0]
    upstream = cotangent[0]
    taps = depth_kernel[0].reshape(TAPS * TAPS * BLOCKS, LANES)
    sources = source_tiles.reshape(4)
    weights = regrid_weights[0].transpose(0, 2, 1)

    (mine,) = run(
        export_kernel, "export", [shape((48, LANES), BF)], state, taps,
        views={1: pl.BlockSpec(memory_space=pl.ANY)},
    )
    fields = lax.ppermute(mine, "group", [(0, 1), (1, 0)])
    one, two = run(
        lon_pack_kernel, "lon_pack", [shape((48, CH), BF)] * 2, state, fields,
        scratch=[vm((48, 384), F32)] * 2,
    )
    one, two = swap_lon(one, two)
    up, down = run(
        lat_pack_kernel, "lat_pack", [shape((224, 384), BF)] * 2, fields, one, two, state,
        scratch=[vm((80, 384), F32)],
    )
    above, below = swap_lat(up, down)
    forced, f_one, f_two = run(
        import_kernel, "import", [shape((CELLS, LANES), BF)] + [shape((48, LANES), BF)] * 2,
        sources, state, weights, fields, one, two, above, below, smem=1,
        scratch=[vm((9, 48, LANES), F32), vm((CELLS, LANES), F32)] + [vm((48, LANES), F32)] * 2
        + [vm((8, CELLS), F32)],
    )
    f_one, f_two = swap_lon(f_one, f_two)
    hidden, update, keep = run(
        conv_wide_kernel, "conv_wide",
        [shape((3, ROWS, COLS, LANES), F32), shape((CELLS, CH), BF), shape((CELLS, LANES), F32)],
        state, one, two, above, below, taps, upstream.reshape(CELLS, CH), land_mask,
        scratch=[vm((3, PAD_ROWS, PAD_COLS, LANES), F32), vm((3, 49, 8, LANES), F32)], room=8,
    )
    f_up, f_down = run(
        rim_pack_kernel, "rim_pack", [shape((176, LANES), BF)] * 2, forced, f_one, f_two, hidden,
        scratch=[vm((32, LANES), F32)], views={3: pl.BlockSpec(memory_space=pl.ANY)},
    )
    f_above, f_below = swap_lat(f_up, f_down)
    normed, hat, inv = run(
        conv_norm_kernel, "conv_norm",
        [shape((ROWS, COLS, CH), BF), shape((ROWS, COLS, CH), F32), shape((ROWS, COLS, LANES), F32)],
        forced, f_one, f_two, f_above, f_below, taps, hidden, norm_gain,
        scratch=[vm((1, PAD_ROWS, PAD_COLS, LANES), F32), vm((1, 49, 8, LANES), F32), vm((ROWS, COLS, LANES), F32)],
        room=6,
    )
    normed = normed.reshape(CELLS, CH)
    hat = hat.reshape(CELLS, CH)
    inv = inv.reshape(CELLS, LANES)

    def half(by_x):
        if by_x:
            dims, block, at = (2, 16, 4, 16, CH), (1, 16, 4, 16, CH), lambda i: (0, 0, 0, 0, 0)
        else:
            dims, block, at = (2, 2, 4, 128, CH), (1, 2, 4, 128, CH), lambda i: (1, 0, 0, 0, 0)
        view = pl.BlockSpec(block, at)
        outs = run(
            functools.partial(mlp_kernel, by_x=by_x), "mlp_x" if by_x else "mlp_y",
            [shape((PART, 2 * CH), BF)] * 4 + [shape((CELLS, HALF), BF)] * 2 + [shape((HALF, CH), BF)] * 2,
            normed, update, w_in[0].reshape(dims), w_out[0].reshape(dims), views={2: view, 3: view}, room=12,
        )
        return outs[:4], outs[4:]

    grads_b, kept_b = half(False)
    grads_b = around(grads_b, "y")
    grads_a, kept_a = half(True)
    a_one, a_two = send(grads_a[1], "x", 1), send(grads_a[2], "x", 2)
    anywhere = pl.BlockSpec(memory_space=pl.ANY)
    d_hidden, d_one, d_two, a_three = run(
        finish_kernel, "finish",
        [shape((CELLS, CH), BF)] + [shape((48, CH), BF)] * 2 + [shape((PART, 2 * CH), BF)],
        kept_a[1], kept_b[1], kept_a[2], kept_b[2], norm_gain, hat, inv, grads_a[3], same={7: 3},
        scratch=[vm((CELLS, CH), F32)] + [vm((48, CH), F32)] * 2, room=12,
    )
    (advanced,) = run(
        advance_kernel, "advance", [shape((CELLS, CH), BF)],
        kept_a[0], kept_b[0], kept_a[3], kept_b[3], state.reshape(CELLS, CH), keep, d_hidden,
        views={6: anywhere}, scratch=[vm((CELLS, CH), F32)], room=12,
    )
    grads_b = run(
        functools.partial(sum_four_kernel, by_x=False), "sum_y", [shape((64, 2 * CH), BF)] * 4,
        *grads_b, advanced, views={4: anywhere}, scratch=[vm((2, 2, 4, 16, 2 * CH), BF)],
    )
    d_one, d_two = swap_lon(d_one, d_two)
    grads_a = [grads_a[0], a_one, a_two, send(a_three, "x", 3)]
    grads_b = around(grads_b, "x")
    grads_a = run(
        functools.partial(sum_four_kernel, by_x=True), "sum_x", [shape((64, 2 * CH), BF)] * 4,
        *grads_a, d_hidden, views={4: anywhere}, scratch=[vm((2, 4, 32, 2 * CH), BF)],
    )
    d_up, d_down = run(
        rim_pack_kernel, "rim_pack_back", [shape((176, CH), BF)] * 2, d_hidden, d_one, d_two, d_one,
        scratch=[vm((32, CH), F32)], views={3: anywhere},
    )
    d_above, d_below = swap_lat(d_up, d_down)
    grads_a = around(grads_a, "y")
    mine, other = run(
        sum_eight_kernel, "sum_xy", [shape((64, 2 * CH), BF)] * 2, *grads_a, *grads_b,
        scratch=[vm((4, 2, 16, 2 * CH), BF)],
    )
    other = send(other, "z_hi", 1)
    (state_grad,) = run(
        conv_back_kernel, "conv_back", [shape((ROWS, COLS, CH), BF)],
        d_hidden, d_one, d_two, d_above, d_below, taps, upstream, mine, views={7: anywhere},
        scratch=[
            vm((BLOCKS, PAD_ROWS, PAD_COLS, LANES), F32), vm((BLOCKS, 49, 8, LANES), F32),
            vm((BLOCKS, ROWS, COLS, LANES), F32),
        ],
        room=10,
    )
    grads = run(
        sum_two_kernel, "sum_z_hi", [shape((16, 2 * CH), BF)] * 4, mine, other, state_grad, views={2: anywhere},
        scratch=[vm((4, 16, 2 * CH), BF)],
    )
    grads = around(grads, "z_lo")
    grad_in, grad_out = run(sum_last_kernel, "sum_z", [shape((16, CH), F32)] * 2, *grads)
    return (
        advanced.reshape(1, ROWS, COLS, CH),
        state_grad[None],
        grad_in[None],
        grad_out[None],
    )


def solution(mesh):
    placed = (
        P("group", "lat", "lon", None),
        P("group", "lat", "lon", None),
        P("group", None, None, None),
        P("group", None),
        P("group", None, None),
        P("group", None, None),
        P("group", "lat", "lon", None),
        P("group", "lat", "lon", None),
        P("lat", "lon"),
    )
    return jax.shard_map(
        body,
        mesh=mesh,
        in_specs=placed,
        out_specs=(
            P("group", "lat", "lon", None),
            P("group", "lat", "lon", None),
            P("group", ("lat", "lon"), None),
            P("group", ("lat", "lon"), None),
        ),
        check_vma=False,
    )
```

```python
import functools

import jax
import jax.numpy as jnp
from jax import lax
from jax.experimental import pallas as pl
from jax.experimental.pallas import tpu as pltpu
from jax.sharding import PartitionSpec as P

Q = 8
EPS = 1e-06
BF = jnp.bfloat16
F32 = jnp.float32
ROWS, COLS, CH, LANES = 16, 48, 512, 128
CELLS = ROWS * COLS
BLOCKS = CH // LANES
RIM = 3
TAPS = 7
LEFT = 8
PAD_ROWS, PAD_COLS = ROWS + 2 * RIM, 64
HALF = 1024
PART = 256
GELU_A = 0.7978845608028654
GELU_B = 0.044715 * GELU_A


def shape(dims, dtype):
    return jax.ShapeDtypeStruct(dims, dtype)


def run(kernel, name, outs, *args, smem=0, scratch=(), views=None, room=4, same=None):
    views = views or {}
    in_specs = [
        pl.BlockSpec(memory_space=pltpu.SMEM)
        if at < smem
        else views.get(at, pl.BlockSpec(memory_space=pltpu.VMEM))
        for at in range(len(args))
    ]
    return pl.pallas_call(
        kernel,
        out_shape=outs,
        grid=(1,),
        in_specs=in_specs,
        out_specs=[pl.BlockSpec(memory_space=pltpu.VMEM)] * len(outs),
        scratch_shapes=list(scratch),
        input_output_aliases=same or {},
        compiler_params=pltpu.CompilerParams(vmem_limit_bytes=room << 20),
        cost_estimate=pl.CostEstimate(flops=0, bytes_accessed=1024, transcendentals=0),
        name=name,
    )(*args)


def lon_is_even():
    return lax.rem(lax.axis_index("lon"), 2) == 0


def cols_into(packed, row, cells, first):
    packed[3 * row : 3 * row + 3, :] = cells[first : first + 3, :]


def by_parity(even, a, b):
    return jnp.where(even, a, b)


def export_kernel(state_ref, out_ref):
    cells = state_ref[:, :, 0:LANES].reshape(CELLS, LANES).astype(F32)
    out_ref[...] = jnp.concatenate(
        [cells[at * LANES : (at + 1) * LANES].T[:Q] for at in range(CELLS // LANES)], axis=0
    ).astype(BF)


def lon_pack_kernel(state_ref, fields_ref, one_ref, two_ref, left, right):
    for row in range(ROWS):
        cols_into(left, row, state_ref[row, 0:16, LANES:].astype(F32), 0)
        cols_into(right, row, state_ref[row, 32:48, LANES:].astype(F32), 13)
    even = lon_is_even()
    one_ref[:, LANES:] = by_parity(even, right[...], left[...]).astype(BF)
    two_ref[:, LANES:] = by_parity(even, left[...], right[...]).astype(BF)
    one_ref[:, :LANES] = fields_ref[...]
    two_ref[:, :LANES] = fields_ref[...]


def sides(one_ref, two_ref):
    even = lon_is_even()
    one, two = one_ref[...].astype(F32), two_ref[...].astype(F32)
    return by_parity(even, two, one), by_parity(even, one, two)


def lat_pack_kernel(fields_ref, one_ref, two_ref, state_ref, up_ref, down_ref, hold):
    up_ref[80:224, :] = state_ref[0:RIM, :, LANES:].reshape(144, 384)
    down_ref[80:224, :] = state_ref[ROWS - RIM :, :, LANES:].reshape(144, 384)
    left, right = sides(one_ref, two_ref)
    hold[0:48, 0:128] = fields_ref[...].astype(F32)
    hold[0:48, 128:256] = left[:, :LANES]
    hold[0:48, 256:384] = right[:, :LANES]
    hold[64:80, :] = jnp.zeros((16, 384), F32)
    for out_ref, at in ((up_ref, 0), (down_ref, 39)):
        hold[48:57, :] = left[at : at + 9, LANES:]
        hold[57:66, :] = right[at : at + 9, LANES:]
        out_ref[0:80, :] = hold[...].astype(BF)


def import_kernel(
    source_ref, state_ref, weight_ref, fields_ref, one_ref, two_ref, above_ref, below_ref, after_ref,
    forced_ref, send_one_ref, send_two_ref, tiles, cells, left, right, flat,
):
    lat, lon = lax.axis_index("lat"), lax.axis_index("lon")
    for row in range(ROWS):
        flat[0:4, row * COLS : (row + 1) * COLS] = weight_ref[row]
    places = []
    for pair in range(4):
        source = source_ref[pair]
        lat_step = source // 32 - lat + 1
        lon_step = lax.rem(lax.rem(source, 32) - lon + 33, 32)
        places.append(jnp.clip(lat_step * 3 + lon_step, 0, 8))
    lon_left, lon_right = sides(one_ref, two_ref)
    tiles[3] = lon_left[:, :LANES]
    tiles[4] = fields_ref[...].astype(F32)
    tiles[5] = lon_right[:, :LANES]
    for at, ref in ((0, above_ref), (6, below_ref)):
        tiles[at + 1] = ref[0:48, 0:128].astype(F32)
        tiles[at] = ref[0:48, 128:256].astype(F32)
        tiles[at + 2] = ref[0:48, 256:384].astype(F32)
    state = state_ref[:, :, 0:LANES].reshape(CELLS, LANES).astype(F32)
    for at in range(CELLS // LANES):
        running = jnp.zeros((Q, LANES), F32)
        for pair in range(4):
            weight = flat[pair : pair + 1, at * LANES : (at + 1) * LANES]
            running = running + weight * tiles[places[pair], at * Q : (at + 1) * Q, :]
        wide = jnp.concatenate(
            [jnp.zeros((Q, LANES), F32), running, jnp.zeros((LANES - 2 * Q, LANES), F32)], axis=0
        )
        cells[at * LANES : (at + 1) * LANES, :] = state[at * LANES : (at + 1) * LANES] + wide.T
    forced_ref[...] = cells[...].astype(BF)
    for row in range(ROWS):
        start = row * COLS
        left[3 * row : 3 * row + 3, :] = cells[start : start + 3, :]
        right[3 * row : 3 * row + 3, :] = cells[start + 45 : start + 48, :]
    even = lon_is_even()
    send_one_ref[...] = by_parity(even, right[...], left[...]).astype(BF)
    send_two_ref[...] = by_parity(even, left[...], right[...]).astype(BF)


def rim_pack_kernel(cells_ref, one_ref, two_ref, after_ref, up_ref, down_ref, hold):
    left, right = sides(one_ref, two_ref)
    width = hold.shape[1]
    hold[16:32, :] = jnp.zeros((16, width), F32)
    for out_ref, first, at in ((up_ref, 0, 0), (down_ref, CELLS - 144, 39)):
        out_ref[0:144, :] = cells_ref[first : first + 144, :]
        hold[0:9, :] = left[at : at + 9]
        hold[9:18, :] = right[at : at + 9]
        out_ref[144:176, :] = hold[...].astype(BF)


def spread_taps(spread, kernel_ref, lane_from, blocks, flipped):
    for at in range(blocks):
        for tap in range(TAPS * TAPS):
            from_tap = TAPS * TAPS - 1 - tap if flipped else tap
            spread[at, tap] = jnp.broadcast_to(kernel_ref[from_tap, lane_from + at : lane_from + at + 1, :], (8, LANES))


def fill_rows(pad, at, top, middle, bottom):
    pad[at, 0:RIM, LEFT : LEFT + COLS, :] = top
    pad[at, RIM : RIM + ROWS, LEFT : LEFT + COLS, :] = middle
    pad[at, RIM + ROWS :, LEFT : LEFT + COLS, :] = bottom


def fill_sides(pad, at, left, right, above, below):
    for row in range(PAD_ROWS):
        if row < RIM:
            one = above[3 * row : 3 * row + 3]
            two = above[9 + 3 * row : 12 + 3 * row]
        elif row < RIM + ROWS:
            one = left[3 * (row - RIM) : 3 * (row - RIM) + 3]
            two = right[3 * (row - RIM) : 3 * (row - RIM) + 3]
        else:
            low = row - RIM - ROWS
            one = below[3 * low : 3 * low + 3]
            two = below[9 + 3 * low : 12 + 3 * low]
        pad[at, row, LEFT - RIM : LEFT, :] = one
        pad[at, row, LEFT + COLS : LEFT + COLS + RIM, :] = two


PASSES = ((0, 1, 2), (3, 4), (5, 6))


def convolve(pad, spread, at, out):
    for first in (0, 24):
        cols = slice(first, first + 24)
        for shifts in PASSES:
            taps = {
                (off, shift): spread[at, off * TAPS + shift][None] for off in range(TAPS) for shift in shifts
            }
            sums = {}
            for row in range(PAD_ROWS):
                start = first + LEFT - RIM
                window = {
                    shift: pad[at, row, start + shift : start + shift + 24, :].reshape(3, 8, LANES)
                    for shift in shifts
                }
                for off in range(TAPS):
                    out_row = row - off
                    if 0 <= out_row < ROWS:
                        part = window[shifts[0]] * taps[off, shifts[0]]
                        for shift in shifts[1:]:
                            part = part + window[shift] * taps[off, shift]
                        if off > 0:
                            part = part + sums[out_row]
                        elif shifts[0] > 0:
                            part = part + out[at, out_row, cols, :].reshape(3, 8, LANES)
                        sums[out_row] = part
                if row >= TAPS - 1:
                    out_row = row - (TAPS - 1)
                    out[at, out_row, cols, :] = sums.pop(out_row).reshape(24, LANES)


def conv_wide_kernel(
    state_ref, one_ref, two_ref, above_ref, below_ref, kernel_ref, after_ref, hidden_ref, pad, spread, *, blocks
):
    left, right = sides(one_ref, two_ref)
    above = above_ref[48:80, :].astype(F32)
    below = below_ref[48:80, :].astype(F32)
    spread_taps(spread, kernel_ref, blocks[0] + 1, len(blocks), False)
    for at, block in enumerate(blocks):
        wide = slice((block + 1) * LANES, (block + 2) * LANES)
        thin = slice(block * LANES, (block + 1) * LANES)
        fill_rows(
            pad, at, above_ref[80:224, thin].astype(F32).reshape(RIM, COLS, LANES),
            state_ref[:, :, wide].astype(F32), below_ref[80:224, thin].astype(F32).reshape(RIM, COLS, LANES),
        )
        fill_sides(pad, at, left[:, wide], right[:, wide], above[:, thin], below[:, thin])

    def one_block(at, carry):
        convolve(pad, spread, at, hidden_ref)
        return carry

    lax.fori_loop(0, len(blocks), one_block, 0)


def d_active_kernel(
    upstream_ref, mask_ref, w_out_ref, after_ref, update_ref, keep_ref, by_x_ref, by_y_ref, token_ref
):
    token_ref[...] = jnp.zeros((8, LANES), F32)
    mask = jnp.where(lax.axis_index("group") == 1, mask_ref[...].astype(F32), 1.0).T
    for row in range(ROWS):
        rows = slice(row * COLS, (row + 1) * COLS)
        keep_ref[rows, :] = jnp.broadcast_to(mask[:, row : row + 1], (COLS, LANES))
    for at in range(BLOCKS):
        lanes = slice(at * LANES, (at + 1) * LANES)
        update_ref[:, lanes] = (keep_ref[...] * upstream_ref[:, lanes].astype(F32)).astype(BF)
    update = update_ref[...]
    for step in range(4):
        mine = slice(step * PART, (step + 1) * PART)
        chunk = lax.rem(along("x") + step, 4)
        by_x_ref[:, mine] = dot(update, w_out_ref[0:16, chunk].reshape(PART, CH), 1, 1)
        chunk = lax.rem(along("y") + step, 4)
        for part in range(2):
            rows = w_out_ref[pl.ds(16 + 8 * part + 2 * chunk, 2)].reshape(LANES, CH)
            spot = slice(step * PART + part * LANES, step * PART + (part + 1) * LANES)
            by_y_ref[:, spot] = dot(update, rows, 1, 1)


def conv_norm_kernel(
    forced_ref, one_ref, two_ref, above_ref, below_ref, kernel_ref, hidden_ref, more_ref, gain_ref,
    normed_ref, hat_ref, inv_ref, pad, spread, first,
):
    left, right = sides(one_ref, two_ref)
    above, below = above_ref[...].astype(F32), below_ref[...].astype(F32)
    spread_taps(spread, kernel_ref, 0, 1, False)
    fill_rows(
        pad, 0, above[0:144].reshape(RIM, COLS, LANES),
        forced_ref[...].astype(F32).reshape(ROWS, COLS, LANES), below[0:144].reshape(RIM, COLS, LANES),
    )
    fill_sides(pad, 0, left, right, above[144:176], below[144:176])

    convolve(pad, spread, 0, first)

    def one_row(row, carry):
        parts = [first[0, row], hidden_ref[0, row], more_ref[0, row], more_ref[1, row]]
        centre = jnp.sum(sum(parts[1:], parts[0]), axis=-1, keepdims=True) * (1.0 / CH)
        parts = [part - centre for part in parts]
        squares = [part * part for part in parts]
        variance = jnp.sum(sum(squares[1:], squares[0]), axis=-1, keepdims=True) * (1.0 / CH)
        inv = lax.rsqrt(variance + EPS)
        inv_ref[row] = jnp.broadcast_to(inv, (COLS, LANES))
        for at in range(BLOCKS):
            lanes = slice(at * LANES, (at + 1) * LANES)
            hat = parts[at] * inv
            hat_ref[row, :, lanes] = hat
            normed_ref[row, :, lanes] = (hat * gain_ref[:, lanes]).astype(BF)
        return carry

    lax.fori_loop(0, ROWS, one_row, 0)


def dot(a, b, left, right):
    return lax.dot_general(a, b, (((left,), (right,)), ((), ())), preferred_element_type=F32)


def along(axis):
    lon = lax.axis_index("lon")
    if axis == "x":
        return lax.rem(lon, 4)
    if axis == "y":
        return lon // 8
    return lax.rem(lon // 4, 2)


def mlp_kernel(
    normed_ref, update_ref, d_active_ref, w_in_ref, w_out_ref,
    grad0_ref, grad1_ref, grad2_ref, grad3_ref, act_ref, pre_ref, w_in_out_ref, w_out_out_ref,
    *, by_x,
):
    normed = normed_ref[...]
    update = update_ref[...]
    for step, grad_ref in enumerate((grad0_ref, grad1_ref, grad2_ref, grad3_ref)):
        chunk = lax.rem(along("x" if by_x else "y") + step, 4)
        first = w_in_ref[0, :, chunk].reshape(PART, CH)
        second = w_out_ref[0, :, chunk].reshape(PART, CH)
        mine = slice(step * PART, (step + 1) * PART)
        w_in_out_ref[mine, :] = first
        w_out_out_ref[mine, :] = second
        value = dot(normed, first, 1, 1)
        square = value * value
        bent = jnp.tanh(value * (GELU_A + GELU_B * square))
        cdf = 0.5 + 0.5 * bent
        act = (value * cdf).astype(BF)
        slope = cdf + (0.5 * value) * (1.0 - bent * bent) * (GELU_A + 3.0 * GELU_B * square)
        pre = (d_active_ref[:, mine] * slope).astype(BF)
        act_ref[:, mine] = act
        pre_ref[:, mine] = pre
        grad_ref[:, :CH] = dot(pre, normed, 0, 0).astype(BF)
        grad_ref[:, CH:] = dot(act, update, 0, 0).astype(BF)


def advance_kernel(
    act_a_ref, act_b_ref, w_out_a_ref, w_out_b_ref, state_ref, keep_ref, after_ref, advanced_ref, token_ref, wide
):
    token_ref[...] = jnp.zeros((8, LANES), F32)
    wide[...] = dot(act_a_ref[...], w_out_a_ref[...], 1, 0) + dot(act_b_ref[...], w_out_b_ref[...], 1, 0)
    for at in range(BLOCKS):
        lanes = slice(at * LANES, (at + 1) * LANES)
        advanced_ref[:, lanes] = (state_ref[:, lanes].astype(F32) + keep_ref[...] * wide[:, lanes]).astype(BF)


def finish_kernel(
    pre_a_ref, pre_b_ref, w_in_a_ref, w_in_b_ref, gain_ref, hat_ref, inv_ref, passed_ref,
    d_hidden_ref, one_ref, two_ref, passed_out_ref, wide, left, right,
):
    wide[...] = dot(pre_a_ref[...], w_in_a_ref[...], 1, 0) + dot(pre_b_ref[...], w_in_b_ref[...], 1, 0)

    def one_row(row, carry):
        rows = pl.ds(pl.multiple_of(row * COLS, COLS), COLS)
        hat = hat_ref[rows, :]
        scaled = wide[rows, :] * gain_ref[...]
        plain = jnp.sum(scaled, axis=-1, keepdims=True) * (1.0 / CH)
        mixed = jnp.sum(scaled * hat, axis=-1, keepdims=True) * (1.0 / CH)
        back = inv_ref[rows, 0:1] * (scaled - plain - hat * mixed)
        wide[rows, :] = back
        d_hidden_ref[rows, :] = back.astype(BF)
        return carry

    lax.fori_loop(0, ROWS, one_row, 0)
    for row in range(ROWS):
        start = row * COLS
        left[3 * row : 3 * row + 3, :] = wide[start : start + 3, :]
        right[3 * row : 3 * row + 3, :] = wide[start + 45 : start + 48, :]
    even = lon_is_even()
    one_ref[...] = by_parity(even, right[...], left[...]).astype(BF)
    two_ref[...] = by_parity(even, left[...], right[...]).astype(BF)


def conv_back_kernel(
    d_hidden_ref, one_ref, two_ref, above_ref, below_ref, kernel_ref, upstream_ref, after_ref,
    out_ref, token_ref, pad, spread, held,
):
    left, right = sides(one_ref, two_ref)
    spread_taps(spread, kernel_ref, 0, BLOCKS, True)
    for at in range(BLOCKS):
        lanes = slice(at * LANES, (at + 1) * LANES)
        above, below = above_ref[:, lanes].astype(F32), below_ref[:, lanes].astype(F32)
        fill_rows(
            pad, at, above[0:144].reshape(RIM, COLS, LANES),
            d_hidden_ref[:, lanes].astype(F32).reshape(ROWS, COLS, LANES),
            below[0:144].reshape(RIM, COLS, LANES),
        )
        fill_sides(pad, at, left[:, lanes], right[:, lanes], above[144:176], below[144:176])

    token_ref[...] = jnp.zeros((8, LANES), F32)

    def one_block(at, carry):
        convolve(pad, spread, at, held)
        return carry

    lax.fori_loop(0, BLOCKS, one_block, 0)
    for at in range(BLOCKS):
        lanes = slice(at * LANES, (at + 1) * LANES)
        out_ref[:, :, lanes] = (upstream_ref[:, :, lanes].astype(F32) + held[at]).astype(BF)


def sum_refs(refs):
    total = refs[0][...].astype(F32)
    for ref in refs[1:]:
        total = total + ref[...].astype(F32)
    return total


def sum_four_kernel(a, b, c, d, after, out0, out1, out2, out3, hold, *, by_x):
    hold[...] = sum_refs((a, b, c, d)).astype(BF).reshape(hold.shape)
    for step, out in enumerate((out0, out1, out2, out3)):
        chunk = lax.rem(along("y" if by_x else "x") + step, 4)
        if by_x:
            out[...] = hold[:, chunk].reshape(out.shape)
        else:
            out[...] = hold[:, :, chunk].reshape(out.shape)


def sum_eight_kernel(*refs):
    ins, (mine, other), hold = refs[:8], refs[8:10], refs[10]
    hold[0:2] = sum_refs(ins[:4]).astype(BF).reshape(2, 2, 16, 2 * CH)
    hold[2:4] = sum_refs(ins[4:]).astype(BF).reshape(2, 2, 16, 2 * CH)
    at = along("z_hi")
    mine[...] = hold[:, at].reshape(64, 2 * CH)
    other[...] = hold[:, 1 - at].reshape(64, 2 * CH)


def sum_two_kernel(a, b, after, out0, out1, out2, out3, hold):
    hold[...] = sum_refs((a, b)).astype(BF).reshape(4, 16, 2 * CH)
    for step, out in enumerate((out0, out1, out2, out3)):
        out[...] = hold[lax.rem(lax.axis_index("lat") + step, 4)]


def sum_last_kernel(*refs):
    total = sum_refs(refs[:4])
    refs[4][...] = total[:, :CH]
    refs[5][...] = total[:, CH:]


def ring(axis):
    if axis == "x":
        lines = [[(i, a, b) for i in range(4)] for a in range(4) for b in range(8)]
    elif axis == "y":
        lines = [[(a, i, b) for i in range(4)] for a in range(4) for b in range(8)]
    elif axis == "z_hi":
        lines = [[(a, b, i + 4 * j) for j in range(2)] for a in range(4) for b in range(4) for i in range(4)]
    else:
        lines = [[(a, b, i + 4 * j) for i in range(4)] for a in range(4) for b in range(4) for j in range(2)]
    return [[(z % 4) * 32 + y * 8 + (z // 4) * 4 + x for x, y, z in line] for line in lines]


def send(piece, axis, step):
    groups = ring(axis)
    count = len(groups[0])
    pairs = [(g[i], g[(i + step) % count]) for g in groups for i in range(count)]
    return lax.ppermute(piece, ("lat", "lon"), pairs)


def around(pieces, axis):
    return [pieces[0]] + [send(piece, axis, step) for step, piece in enumerate(pieces) if step]


def swap_lon(one, two):
    pairs = [(i, i ^ 1) for i in range(32)]
    other = [(i, (i - 1) % 32 if i % 2 == 0 else (i + 1) % 32) for i in range(32)]
    two = lax.ppermute(two, "lon", other)
    return lax.ppermute(one, "lon", pairs), two


def swap_lat(up, down):
    above = lax.ppermute(down, "lat", [(i, i + 1) for i in range(3)])
    below = lax.ppermute(up, "lat", [(i + 1, i) for i in range(3)])
    return above, below


def body(
    states, cotangent, depth_kernel, norm_gain, w_in, w_out, source_tiles, regrid_weights, land_mask
):
    vm = pltpu.VMEM
    state = states[0]
    upstream = cotangent[0]
    taps = depth_kernel[0].reshape(TAPS * TAPS, BLOCKS, LANES)
    sources = source_tiles.reshape(4)
    weights = regrid_weights[0].transpose(0, 2, 1)

    (mine,) = run(
        export_kernel, "export", [shape((48, LANES), BF)], state,
    )
    fields = lax.ppermute(mine, "group", [(0, 1), (1, 0)])
    one, two = run(
        lon_pack_kernel, "lon_pack", [shape((48, CH), BF)] * 2, state, fields,
        scratch=[vm((48, 384), F32)] * 2,
    )
    one, two = swap_lon(one, two)
    up, down = run(
        lat_pack_kernel, "lat_pack", [shape((224, 384), BF)] * 2, fields, one, two, state,
        scratch=[vm((80, 384), F32)],
    )
    above, below = swap_lat(up, down)
    anywhere = pl.BlockSpec(memory_space=pl.ANY)
    update, keep, by_x, by_y, token = run(
        d_active_kernel, "d_active",
        [shape((CELLS, CH), BF), shape((CELLS, LANES), F32)] + [shape((CELLS, HALF), F32)] * 2
        + [shape((8, LANES), F32)],
        upstream.reshape(CELLS, CH), land_mask, w_out[0].reshape(32, 4, 16, CH), up, views={3: anywhere}, room=12,
    )
    forced, f_one, f_two = run(
        import_kernel, "import", [shape((CELLS, LANES), BF)] + [shape((48, LANES), BF)] * 2,
        sources, state, weights, fields, one, two, above, below, token, smem=1, views={8: anywhere},
        scratch=[vm((9, 48, LANES), F32), vm((CELLS, LANES), F32)] + [vm((48, LANES), F32)] * 2
        + [vm((8, CELLS), F32)],
    )
    f_one, f_two = swap_lon(f_one, f_two)
    (hidden,) = run(
        functools.partial(conv_wide_kernel, blocks=(0,)), "conv_one", [shape((1, ROWS, COLS, LANES), F32)],
        state, one, two, above, below, taps, forced, views={6: anywhere},
        scratch=[vm((1, PAD_ROWS, PAD_COLS, LANES), F32), vm((1, 49, 8, LANES), F32)], room=6,
    )
    f_up, f_down = run(
        rim_pack_kernel, "rim_pack", [shape((176, LANES), BF)] * 2, forced, f_one, f_two, hidden,
        scratch=[vm((32, LANES), F32)], views={3: pl.BlockSpec(memory_space=pl.ANY)},
    )
    f_above, f_below = swap_lat(f_up, f_down)
    (more,) = run(
        functools.partial(conv_wide_kernel, blocks=(1, 2)), "conv_two", [shape((2, ROWS, COLS, LANES), F32)],
        state, one, two, above, below, taps, f_up, views={6: anywhere},
        scratch=[vm((2, PAD_ROWS, PAD_COLS, LANES), F32), vm((2, 49, 8, LANES), F32)], room=6,
    )
    normed, hat, inv = run(
        conv_norm_kernel, "conv_norm",
        [shape((ROWS, COLS, CH), BF), shape((ROWS, COLS, CH), F32), shape((ROWS, COLS, LANES), F32)],
        forced, f_one, f_two, f_above, f_below, taps, hidden, more, norm_gain,
        scratch=[vm((1, PAD_ROWS, PAD_COLS, LANES), F32), vm((1, 49, 8, LANES), F32), vm((1, ROWS, COLS, LANES), F32)],
        room=6,
    )
    normed = normed.reshape(CELLS, CH)
    hat = hat.reshape(CELLS, CH)
    inv = inv.reshape(CELLS, LANES)

    def half(by_x, d_active):
        if by_x:
            dims, block, at = (2, 16, 4, 16, CH), (1, 16, 4, 16, CH), lambda i: (0, 0, 0, 0, 0)
        else:
            dims, block, at = (2, 2, 4, 128, CH), (1, 2, 4, 128, CH), lambda i: (1, 0, 0, 0, 0)
        view = pl.BlockSpec(block, at)
        outs = run(
            functools.partial(mlp_kernel, by_x=by_x), "mlp_x" if by_x else "mlp_y",
            [shape((PART, 2 * CH), BF)] * 4 + [shape((CELLS, HALF), BF)] * 2 + [shape((HALF, CH), BF)] * 2,
            normed, update, d_active, w_in[0].reshape(dims), w_out[0].reshape(dims), views={3: view, 4: view}, room=12,
        )
        return outs[:4], outs[4:]

    grads_b, kept_b = half(False, by_y)
    grads_b = around(grads_b, "y")
    grads_a, kept_a = half(True, by_x)
    a_one, a_two = send(grads_a[1], "x", 1), send(grads_a[2], "x", 2)
    d_hidden, d_one, d_two, a_three = run(
        finish_kernel, "finish",
        [shape((CELLS, CH), BF)] + [shape((48, CH), BF)] * 2 + [shape((PART, 2 * CH), BF)],
        kept_a[1], kept_b[1], kept_a[2], kept_b[2], norm_gain, hat, inv, grads_a[3], same={7: 3},
        scratch=[vm((CELLS, CH), F32)] + [vm((48, CH), F32)] * 2, room=12,
    )
    advanced, token = run(
        advance_kernel, "advance", [shape((CELLS, CH), BF), shape((8, LANES), F32)],
        kept_a[0], kept_b[0], kept_a[3], kept_b[3], state.reshape(CELLS, CH), keep, d_hidden,
        views={6: anywhere}, scratch=[vm((CELLS, CH), F32)], room=12,
    )
    grads_b = run(
        functools.partial(sum_four_kernel, by_x=False), "sum_y", [shape((64, 2 * CH), BF)] * 4,
        *grads_b, token, views={4: anywhere}, scratch=[vm((2, 2, 4, 16, 2 * CH), BF)],
    )
    d_one, d_two = swap_lon(d_one, d_two)
    grads_a = [grads_a[0], a_one, a_two, send(a_three, "x", 3)]
    grads_b = around(grads_b, "x")
    grads_a = run(
        functools.partial(sum_four_kernel, by_x=True), "sum_x", [shape((64, 2 * CH), BF)] * 4,
        *grads_a, d_hidden, views={4: anywhere}, scratch=[vm((2, 4, 32, 2 * CH), BF)],
    )
    d_up, d_down = run(
        rim_pack_kernel, "rim_pack_back", [shape((176, CH), BF)] * 2, d_hidden, d_one, d_two, d_one,
        scratch=[vm((32, CH), F32)], views={3: anywhere},
    )
    d_above, d_below = swap_lat(d_up, d_down)
    grads_a = around(grads_a, "y")
    mine, other = run(
        sum_eight_kernel, "sum_xy", [shape((64, 2 * CH), BF)] * 2, *grads_a, *grads_b,
        scratch=[vm((4, 2, 16, 2 * CH), BF)],
    )
    other = send(other, "z_hi", 1)
    state_grad, token = run(
        conv_back_kernel, "conv_back", [shape((ROWS, COLS, CH), BF), shape((8, LANES), F32)],
        d_hidden, d_one, d_two, d_above, d_below, taps, upstream, mine, views={7: anywhere},
        scratch=[
            vm((BLOCKS, PAD_ROWS, PAD_COLS, LANES), F32), vm((BLOCKS, 49, 8, LANES), F32),
            vm((BLOCKS, ROWS, COLS, LANES), F32),
        ],
        room=10,
    )
    grads = run(
        sum_two_kernel, "sum_z_hi", [shape((16, 2 * CH), BF)] * 4, mine, other, token, views={2: anywhere},
        scratch=[vm((4, 16, 2 * CH), BF)],
    )
    grads = around(grads, "z_lo")
    grad_in, grad_out = run(sum_last_kernel, "sum_z", [shape((16, CH), F32)] * 2, *grads)
    return (
        advanced.reshape(1, ROWS, COLS, CH),
        state_grad[None],
        grad_in[None],
        grad_out[None],
    )


def solution(mesh):
    placed = (
        P("group", "lat", "lon", None),
        P("group", "lat", "lon", None),
        P("group", None, None, None),
        P("group", None),
        P("group", None, None),
        P("group", None, None),
        P("group", "lat", "lon", None),
        P("group", "lat", "lon", None),
        P("lat", "lon"),
    )
    return jax.shard_map(
        body,
        mesh=mesh,
        in_specs=placed,
        out_specs=(
            P("group", "lat", "lon", None),
            P("group", "lat", "lon", None),
            P("group", ("lat", "lon"), None),
            P("group", ("lat", "lon"), None),
        ),
        check_vma=False,
    )
```

```python
import functools

import jax
import jax.numpy as jnp
from jax import lax
from jax.experimental import pallas as pl
from jax.experimental.pallas import tpu as pltpu
from jax.sharding import PartitionSpec as P

Q = 8
EPS = 1e-06
BF = jnp.bfloat16
F32 = jnp.float32
ROWS, COLS, CH, LANES = 16, 48, 512, 128
CELLS = ROWS * COLS
BLOCKS = CH // LANES
RIM = 3
TAPS = 7
LEFT = 8
PAD_ROWS, PAD_COLS = ROWS + 2 * RIM, 64
HALF = 1024
PART = 256
GELU_A = 0.7978845608028654
GELU_B = 0.044715 * GELU_A


def shape(dims, dtype):
    return jax.ShapeDtypeStruct(dims, dtype)


def run(kernel, name, outs, *args, smem=0, scratch=(), views=None, room=4, same=None):
    views = views or {}
    in_specs = [
        pl.BlockSpec(memory_space=pltpu.SMEM)
        if at < smem
        else views.get(at, pl.BlockSpec(memory_space=pltpu.VMEM))
        for at in range(len(args))
    ]
    return pl.pallas_call(
        kernel,
        out_shape=outs,
        grid=(1,),
        in_specs=in_specs,
        out_specs=[pl.BlockSpec(memory_space=pltpu.VMEM)] * len(outs),
        scratch_shapes=list(scratch),
        input_output_aliases=same or {},
        compiler_params=pltpu.CompilerParams(vmem_limit_bytes=room << 20),
        cost_estimate=pl.CostEstimate(flops=0, bytes_accessed=1024, transcendentals=0),
        name=name,
    )(*args)


def lon_is_even():
    return lax.rem(lax.axis_index("lon"), 2) == 0


def cols_into(packed, row, cells, first):
    packed[3 * row : 3 * row + 3, :] = cells[first : first + 3, :]


def by_parity(even, a, b):
    return jnp.where(even, a, b)


def export_kernel(state_ref, out_ref):
    cells = state_ref[:, :, 0:LANES].reshape(CELLS, LANES).astype(F32)
    out_ref[...] = jnp.concatenate(
        [cells[at * LANES : (at + 1) * LANES].T[:Q] for at in range(CELLS // LANES)], axis=0
    ).astype(BF)


def lon_pack_kernel(state_ref, fields_ref, one_ref, two_ref, left, right):
    for row in range(ROWS):
        cols_into(left, row, state_ref[row, 0:16, LANES:].astype(F32), 0)
        cols_into(right, row, state_ref[row, 32:48, LANES:].astype(F32), 13)
    even = lon_is_even()
    one_ref[:, LANES:] = by_parity(even, right[...], left[...]).astype(BF)
    two_ref[:, LANES:] = by_parity(even, left[...], right[...]).astype(BF)
    one_ref[:, :LANES] = fields_ref[...]
    two_ref[:, :LANES] = fields_ref[...]


def sides(one_ref, two_ref):
    even = lon_is_even()
    one, two = one_ref[...].astype(F32), two_ref[...].astype(F32)
    return by_parity(even, two, one), by_parity(even, one, two)


def lat_pack_kernel(fields_ref, one_ref, two_ref, state_ref, up_ref, down_ref, hold):
    up_ref[80:224, :] = state_ref[0:RIM, :, LANES:].reshape(144, 384)
    down_ref[80:224, :] = state_ref[ROWS - RIM :, :, LANES:].reshape(144, 384)
    left, right = sides(one_ref, two_ref)
    hold[0:48, 0:128] = fields_ref[...].astype(F32)
    hold[0:48, 128:256] = left[:, :LANES]
    hold[0:48, 256:384] = right[:, :LANES]
    hold[64:80, :] = jnp.zeros((16, 384), F32)
    for out_ref, at in ((up_ref, 0), (down_ref, 39)):
        hold[48:57, :] = left[at : at + 9, LANES:]
        hold[57:66, :] = right[at : at + 9, LANES:]
        out_ref[0:80, :] = hold[...].astype(BF)


def import_kernel(
    source_ref, state_ref, weight_ref, fields_ref, one_ref, two_ref, above_ref, below_ref,
    forced_ref, send_one_ref, send_two_ref, tiles, cells, left, right, flat,
):
    lat, lon = lax.axis_index("lat"), lax.axis_index("lon")
    for row in range(ROWS):
        flat[0:4, row * COLS : (row + 1) * COLS] = weight_ref[row]
    places = []
    for pair in range(4):
        source = source_ref[pair]
        lat_step = source // 32 - lat + 1
        lon_step = lax.rem(lax.rem(source, 32) - lon + 33, 32)
        places.append(jnp.clip(lat_step * 3 + lon_step, 0, 8))
    lon_left, lon_right = sides(one_ref, two_ref)
    tiles[3] = lon_left[:, :LANES]
    tiles[4] = fields_ref[...].astype(F32)
    tiles[5] = lon_right[:, :LANES]
    for at, ref in ((0, above_ref), (6, below_ref)):
        tiles[at + 1] = ref[0:48, 0:128].astype(F32)
        tiles[at] = ref[0:48, 128:256].astype(F32)
        tiles[at + 2] = ref[0:48, 256:384].astype(F32)
    state = state_ref[:, :, 0:LANES].reshape(CELLS, LANES).astype(F32)
    for at in range(CELLS // LANES):
        running = jnp.zeros((Q, LANES), F32)
        for pair in range(4):
            weight = flat[pair : pair + 1, at * LANES : (at + 1) * LANES]
            running = running + weight * tiles[places[pair], at * Q : (at + 1) * Q, :]
        wide = jnp.concatenate(
            [jnp.zeros((Q, LANES), F32), running, jnp.zeros((LANES - 2 * Q, LANES), F32)], axis=0
        )
        cells[at * LANES : (at + 1) * LANES, :] = state[at * LANES : (at + 1) * LANES] + wide.T
    forced_ref[...] = cells[...].astype(BF)
    for row in range(ROWS):
        start = row * COLS
        left[3 * row : 3 * row + 3, :] = cells[start : start + 3, :]
        right[3 * row : 3 * row + 3, :] = cells[start + 45 : start + 48, :]
    even = lon_is_even()
    send_one_ref[...] = by_parity(even, right[...], left[...]).astype(BF)
    send_two_ref[...] = by_parity(even, left[...], right[...]).astype(BF)


def rim_pack_kernel(cells_ref, one_ref, two_ref, after_ref, up_ref, down_ref, hold):
    left, right = sides(one_ref, two_ref)
    width = hold.shape[1]
    hold[16:32, :] = jnp.zeros((16, width), F32)
    for out_ref, first, at in ((up_ref, 0, 0), (down_ref, CELLS - 144, 39)):
        out_ref[0:144, :] = cells_ref[first : first + 144, :]
        hold[0:9, :] = left[at : at + 9]
        hold[9:18, :] = right[at : at + 9]
        out_ref[144:176, :] = hold[...].astype(BF)


def spread_taps(spread, kernel_ref, lane_from, blocks, flipped):
    for at in range(blocks):
        for tap in range(TAPS * TAPS):
            from_tap = TAPS * TAPS - 1 - tap if flipped else tap
            spread[at, tap] = jnp.broadcast_to(kernel_ref[from_tap, lane_from + at : lane_from + at + 1, :], (8, LANES))


def fill_rows(pad, at, top, middle, bottom):
    pad[at, 0:RIM, LEFT : LEFT + COLS, :] = top
    pad[at, RIM : RIM + ROWS, LEFT : LEFT + COLS, :] = middle
    pad[at, RIM + ROWS :, LEFT : LEFT + COLS, :] = bottom


def fill_sides(pad, at, left, right, above, below):
    for row in range(PAD_ROWS):
        if row < RIM:
            one = above[3 * row : 3 * row + 3]
            two = above[9 + 3 * row : 12 + 3 * row]
        elif row < RIM + ROWS:
            one = left[3 * (row - RIM) : 3 * (row - RIM) + 3]
            two = right[3 * (row - RIM) : 3 * (row - RIM) + 3]
        else:
            low = row - RIM - ROWS
            one = below[3 * low : 3 * low + 3]
            two = below[9 + 3 * low : 12 + 3 * low]
        pad[at, row, LEFT - RIM : LEFT, :] = one
        pad[at, row, LEFT + COLS : LEFT + COLS + RIM, :] = two


PASSES = ((0, 1, 2), (3, 4), (5, 6))


def convolve(pad, spread, at, out):
    for first in (0, 24):
        cols = slice(first, first + 24)
        for shifts in PASSES:
            taps = {
                (off, shift): spread[at, off * TAPS + shift][None] for off in range(TAPS) for shift in shifts
            }
            sums = {}
            for row in range(PAD_ROWS):
                start = first + LEFT - RIM
                window = {
                    shift: pad[at, row, start + shift : start + shift + 24, :].reshape(3, 8, LANES)
                    for shift in shifts
                }
                for off in range(TAPS):
                    out_row = row - off
                    if 0 <= out_row < ROWS:
                        part = window[shifts[0]] * taps[off, shifts[0]]
                        for shift in shifts[1:]:
                            part = part + window[shift] * taps[off, shift]
                        if off > 0:
                            part = part + sums[out_row]
                        elif shifts[0] > 0:
                            part = part + out[at, out_row, cols, :].reshape(3, 8, LANES)
                        sums[out_row] = part
                if row >= TAPS - 1:
                    out_row = row - (TAPS - 1)
                    out[at, out_row, cols, :] = sums.pop(out_row).reshape(24, LANES)


def conv_wide_kernel(
    state_ref, one_ref, two_ref, above_ref, below_ref, kernel_ref, after_ref, hidden_ref, pad, spread, *, blocks
):
    left, right = sides(one_ref, two_ref)
    above = above_ref[48:80, :].astype(F32)
    below = below_ref[48:80, :].astype(F32)
    spread_taps(spread, kernel_ref, blocks[0] + 1, len(blocks), False)
    for at, block in enumerate(blocks):
        wide = slice((block + 1) * LANES, (block + 2) * LANES)
        thin = slice(block * LANES, (block + 1) * LANES)
        fill_rows(
            pad, at, above_ref[80:224, thin].astype(F32).reshape(RIM, COLS, LANES),
            state_ref[:, :, wide].astype(F32), below_ref[80:224, thin].astype(F32).reshape(RIM, COLS, LANES),
        )
        fill_sides(pad, at, left[:, wide], right[:, wide], above[:, thin], below[:, thin])

    def one_block(at, carry):
        convolve(pad, spread, at, hidden_ref)
        return carry

    lax.fori_loop(0, len(blocks), one_block, 0)


def masked_kernel(upstream_ref, mask_ref, after_ref, update_ref, keep_ref):
    mask = jnp.where(lax.axis_index("group") == 1, mask_ref[...].astype(F32), 1.0).T
    for row in range(ROWS):
        rows = slice(row * COLS, (row + 1) * COLS)
        keep_ref[rows, :] = jnp.broadcast_to(mask[:, row : row + 1], (COLS, LANES))
    for at in range(BLOCKS):
        lanes = slice(at * LANES, (at + 1) * LANES)
        update_ref[:, lanes] = (keep_ref[...] * upstream_ref[:, lanes].astype(F32)).astype(BF)


def conv_norm_kernel(
    forced_ref, one_ref, two_ref, above_ref, below_ref, kernel_ref, hidden_ref, more_ref, gain_ref,
    normed_ref, hat_ref, inv_ref, pad, spread, first,
):
    left, right = sides(one_ref, two_ref)
    above, below = above_ref[...].astype(F32), below_ref[...].astype(F32)
    spread_taps(spread, kernel_ref, 0, 1, False)
    fill_rows(
        pad, 0, above[0:144].reshape(RIM, COLS, LANES),
        forced_ref[...].astype(F32).reshape(ROWS, COLS, LANES), below[0:144].reshape(RIM, COLS, LANES),
    )
    fill_sides(pad, 0, left, right, above[144:176], below[144:176])

    convolve(pad, spread, 0, first)

    def one_row(row, carry):
        parts = [first[0, row], hidden_ref[0, row], more_ref[0, row], more_ref[1, row]]
        centre = jnp.sum(sum(parts[1:], parts[0]), axis=-1, keepdims=True) * (1.0 / CH)
        parts = [part - centre for part in parts]
        squares = [part * part for part in parts]
        variance = jnp.sum(sum(squares[1:], squares[0]), axis=-1, keepdims=True) * (1.0 / CH)
        inv = lax.rsqrt(variance + EPS)
        inv_ref[row] = jnp.broadcast_to(inv, (COLS, LANES))
        for at in range(BLOCKS):
            lanes = slice(at * LANES, (at + 1) * LANES)
            hat = parts[at] * inv
            hat_ref[row, :, lanes] = hat
            normed_ref[row, :, lanes] = (hat * gain_ref[:, lanes]).astype(BF)
        return carry

    lax.fori_loop(0, ROWS, one_row, 0, unroll=4)


def dot(a, b, left, right):
    return lax.dot_general(a, b, (((left,), (right,)), ((), ())), preferred_element_type=F32)


def along(axis):
    lon = lax.axis_index("lon")
    if axis == "x":
        return lax.rem(lon, 4)
    if axis == "y":
        return lon // 8
    return lax.rem(lon // 4, 2)


def mlp_kernel(
    normed_ref, update_ref, w_in_ref, w_out_ref,
    grad0_ref, grad1_ref, grad2_ref, grad3_ref, act_ref, pre_ref, w_in_out_ref, w_out_out_ref,
    *, by_x,
):
    def units(step):
        return slice(step * PART, (step + 1) * PART)

    for step in range(4):
        chunk = lax.rem(along("x" if by_x else "y") + step, 4)
        w_in_out_ref[units(step), :] = w_in_ref[0, :, chunk].reshape(PART, CH)
        w_out_out_ref[units(step), :] = w_out_ref[0, :, chunk].reshape(PART, CH)

    def expand(step, rows):
        value = dot(normed_ref[rows, :], w_in_out_ref[units(step), :], 1, 1)
        return value, dot(update_ref[rows, :], w_out_out_ref[units(step), :], 1, 1)

    def bend(step, rows, value, back):
        square = value * value
        bent = jnp.tanh(value * (GELU_A + GELU_B * square))
        cdf = 0.5 + 0.5 * bent
        act_ref[rows, units(step)] = (value * cdf).astype(BF)
        slope = cdf + (0.5 * value) * (1.0 - bent * bent) * (GELU_A + 3.0 * GELU_B * square)
        pre_ref[rows, units(step)] = (back * slope).astype(BF)

    grads = (grad0_ref, grad1_ref, grad2_ref, grad3_ref)
    pieces = [(step, slice(at, at + 256)) for step in range(4) for at in range(0, CELLS, 256)]
    held = expand(*pieces[0])
    for at, (step, rows) in enumerate(pieces):
        following = expand(*pieces[at + 1]) if at + 1 < len(pieces) else None
        bend(step, rows, *held)
        held = following
        if rows.stop == CELLS:
            grads[step][:, :CH] = dot(pre_ref[:, units(step)], normed_ref[...], 0, 0).astype(BF)
            grads[step][:, CH:] = dot(act_ref[:, units(step)], update_ref[...], 0, 0).astype(BF)


def advance_kernel(
    act_a_ref, act_b_ref, w_out_a_ref, w_out_b_ref, state_ref, keep_ref, after_ref, advanced_ref, token_ref, wide
):
    token_ref[...] = jnp.zeros((8, LANES), F32)
    wide[...] = dot(act_a_ref[...], w_out_a_ref[...], 1, 0) + dot(act_b_ref[...], w_out_b_ref[...], 1, 0)
    for at in range(BLOCKS):
        lanes = slice(at * LANES, (at + 1) * LANES)
        advanced_ref[:, lanes] = (state_ref[:, lanes].astype(F32) + keep_ref[...] * wide[:, lanes]).astype(BF)


def finish_kernel(
    pre_a_ref, pre_b_ref, w_in_a_ref, w_in_b_ref, gain_ref, hat_ref, inv_ref, passed_ref,
    d_hidden_ref, one_ref, two_ref, passed_out_ref, wide, left, right,
):
    wide[...] = dot(pre_a_ref[...], w_in_a_ref[...], 1, 0) + dot(pre_b_ref[...], w_in_b_ref[...], 1, 0)

    def one_row(row, carry):
        rows = pl.ds(pl.multiple_of(row * COLS, COLS), COLS)
        hat = hat_ref[rows, :]
        scaled = wide[rows, :] * gain_ref[...]
        plain = jnp.sum(scaled, axis=-1, keepdims=True) * (1.0 / CH)
        mixed = jnp.sum(scaled * hat, axis=-1, keepdims=True) * (1.0 / CH)
        back = inv_ref[rows, 0:1] * (scaled - plain - hat * mixed)
        wide[rows, :] = back
        d_hidden_ref[rows, :] = back.astype(BF)
        return carry

    lax.fori_loop(0, ROWS, one_row, 0, unroll=4)
    for row in range(ROWS):
        start = row * COLS
        left[3 * row : 3 * row + 3, :] = wide[start : start + 3, :]
        right[3 * row : 3 * row + 3, :] = wide[start + 45 : start + 48, :]
    even = lon_is_even()
    one_ref[...] = by_parity(even, right[...], left[...]).astype(BF)
    two_ref[...] = by_parity(even, left[...], right[...]).astype(BF)


def conv_back_kernel(
    d_hidden_ref, one_ref, two_ref, above_ref, below_ref, kernel_ref, upstream_ref, after_ref,
    out_ref, token_ref, pad, spread, held,
):
    left, right = sides(one_ref, two_ref)
    spread_taps(spread, kernel_ref, 0, BLOCKS, True)
    for at in range(BLOCKS):
        lanes = slice(at * LANES, (at + 1) * LANES)
        above, below = above_ref[:, lanes].astype(F32), below_ref[:, lanes].astype(F32)
        fill_rows(
            pad, at, above[0:144].reshape(RIM, COLS, LANES),
            d_hidden_ref[:, lanes].astype(F32).reshape(ROWS, COLS, LANES),
            below[0:144].reshape(RIM, COLS, LANES),
        )
        fill_sides(pad, at, left[:, lanes], right[:, lanes], above[144:176], below[144:176])

    token_ref[...] = jnp.zeros((8, LANES), F32)

    def one_block(at, carry):
        convolve(pad, spread, at, held)
        return carry

    lax.fori_loop(0, BLOCKS, one_block, 0)
    for at in range(BLOCKS):
        lanes = slice(at * LANES, (at + 1) * LANES)
        out_ref[:, :, lanes] = (upstream_ref[:, :, lanes].astype(F32) + held[at]).astype(BF)


def sum_refs(refs):
    total = refs[0][...].astype(F32)
    for ref in refs[1:]:
        total = total + ref[...].astype(F32)
    return total


def sum_four_kernel(a, b, c, d, after, out0, out1, out2, out3, hold, *, by_x):
    hold[...] = sum_refs((a, b, c, d)).astype(BF).reshape(hold.shape)
    for step, out in enumerate((out0, out1, out2, out3)):
        chunk = lax.rem(along("y" if by_x else "x") + step, 4)
        if by_x:
            out[...] = hold[:, chunk].reshape(out.shape)
        else:
            out[...] = hold[:, :, chunk].reshape(out.shape)


def sum_eight_kernel(*refs):
    ins, (mine, other), hold = refs[:8], refs[8:10], refs[10]
    hold[0:2] = sum_refs(ins[:4]).astype(BF).reshape(2, 2, 16, 2 * CH)
    hold[2:4] = sum_refs(ins[4:]).astype(BF).reshape(2, 2, 16, 2 * CH)
    at = along("z_hi")
    mine[...] = hold[:, at].reshape(64, 2 * CH)
    other[...] = hold[:, 1 - at].reshape(64, 2 * CH)


def sum_two_kernel(a, b, after, out0, out1, out2, out3, hold):
    hold[...] = sum_refs((a, b)).astype(BF).reshape(4, 16, 2 * CH)
    for step, out in enumerate((out0, out1, out2, out3)):
        out[...] = hold[lax.rem(lax.axis_index("lat") + step, 4)]


def sum_last_kernel(*refs):
    total = sum_refs(refs[:4])
    refs[4][...] = total[:, :CH]
    refs[5][...] = total[:, CH:]


def ring(axis):
    if axis == "x":
        lines = [[(i, a, b) for i in range(4)] for a in range(4) for b in range(8)]
    elif axis == "y":
        lines = [[(a, i, b) for i in range(4)] for a in range(4) for b in range(8)]
    elif axis == "z_hi":
        lines = [[(a, b, i + 4 * j) for j in range(2)] for a in range(4) for b in range(4) for i in range(4)]
    else:
        lines = [[(a, b, i + 4 * j) for i in range(4)] for a in range(4) for b in range(4) for j in range(2)]
    return [[(z % 4) * 32 + y * 8 + (z // 4) * 4 + x for x, y, z in line] for line in lines]


def send(piece, axis, step):
    groups = ring(axis)
    count = len(groups[0])
    pairs = [(g[i], g[(i + step) % count]) for g in groups for i in range(count)]
    return lax.ppermute(piece, ("lat", "lon"), pairs)


def around(pieces, axis):
    return [pieces[0]] + [send(piece, axis, step) for step, piece in enumerate(pieces) if step]


def swap_lon(one, two):
    pairs = [(i, i ^ 1) for i in range(32)]
    other = [(i, (i - 1) % 32 if i % 2 == 0 else (i + 1) % 32) for i in range(32)]
    two = lax.ppermute(two, "lon", other)
    return lax.ppermute(one, "lon", pairs), two


def swap_lat(up, down):
    above = lax.ppermute(down, "lat", [(i, i + 1) for i in range(3)])
    below = lax.ppermute(up, "lat", [(i + 1, i) for i in range(3)])
    return above, below


def body(
    states, cotangent, depth_kernel, norm_gain, w_in, w_out, source_tiles, regrid_weights, land_mask
):
    vm = pltpu.VMEM
    state = states[0]
    upstream = cotangent[0]
    taps = depth_kernel[0].reshape(TAPS * TAPS, BLOCKS, LANES)
    sources = source_tiles.reshape(4)
    weights = regrid_weights[0].transpose(0, 2, 1)

    (mine,) = run(
        export_kernel, "export", [shape((48, LANES), BF)], state,
    )
    fields = lax.ppermute(mine, "group", [(0, 1), (1, 0)])
    one, two = run(
        lon_pack_kernel, "lon_pack", [shape((48, CH), BF)] * 2, state, fields,
        scratch=[vm((48, 384), F32)] * 2,
    )
    one, two = swap_lon(one, two)
    up, down = run(
        lat_pack_kernel, "lat_pack", [shape((224, 384), BF)] * 2, fields, one, two, state,
        scratch=[vm((80, 384), F32)],
    )
    above, below = swap_lat(up, down)
    anywhere = pl.BlockSpec(memory_space=pl.ANY)
    forced, f_one, f_two = run(
        import_kernel, "import", [shape((CELLS, LANES), BF)] + [shape((48, LANES), BF)] * 2,
        sources, state, weights, fields, one, two, above, below, smem=1,
        scratch=[vm((9, 48, LANES), F32), vm((CELLS, LANES), F32)] + [vm((48, LANES), F32)] * 2
        + [vm((8, CELLS), F32)],
    )
    f_one, f_two = swap_lon(f_one, f_two)
    update, keep = run(
        masked_kernel, "masked", [shape((CELLS, CH), BF), shape((CELLS, LANES), F32)],
        upstream.reshape(CELLS, CH), land_mask, forced, views={2: anywhere},
    )
    (hidden,) = run(
        functools.partial(conv_wide_kernel, blocks=(0,)), "conv_one", [shape((1, ROWS, COLS, LANES), F32)],
        state, one, two, above, below, taps, keep, views={6: anywhere},
        scratch=[vm((1, PAD_ROWS, PAD_COLS, LANES), F32), vm((1, 49, 8, LANES), F32)], room=6,
    )
    f_up, f_down = run(
        rim_pack_kernel, "rim_pack", [shape((176, LANES), BF)] * 2, forced, f_one, f_two, hidden,
        scratch=[vm((32, LANES), F32)], views={3: pl.BlockSpec(memory_space=pl.ANY)},
    )
    f_above, f_below = swap_lat(f_up, f_down)
    (more,) = run(
        functools.partial(conv_wide_kernel, blocks=(1, 2)), "conv_two", [shape((2, ROWS, COLS, LANES), F32)],
        state, one, two, above, below, taps, f_up, views={6: anywhere},
        scratch=[vm((2, PAD_ROWS, PAD_COLS, LANES), F32), vm((2, 49, 8, LANES), F32)], room=6,
    )
    normed, hat, inv = run(
        conv_norm_kernel, "conv_norm",
        [shape((ROWS, COLS, CH), BF), shape((ROWS, COLS, CH), F32), shape((ROWS, COLS, LANES), F32)],
        forced, f_one, f_two, f_above, f_below, taps, hidden, more, norm_gain,
        scratch=[vm((1, PAD_ROWS, PAD_COLS, LANES), F32), vm((1, 49, 8, LANES), F32), vm((1, ROWS, COLS, LANES), F32)],
        room=6,
    )
    normed = normed.reshape(CELLS, CH)
    hat = hat.reshape(CELLS, CH)
    inv = inv.reshape(CELLS, LANES)

    def half(by_x):
        if by_x:
            dims, block, at = (2, 16, 4, 16, CH), (1, 16, 4, 16, CH), lambda i: (0, 0, 0, 0, 0)
        else:
            dims, block, at = (2, 2, 4, 128, CH), (1, 2, 4, 128, CH), lambda i: (1, 0, 0, 0, 0)
        view = pl.BlockSpec(block, at)
        outs = run(
            functools.partial(mlp_kernel, by_x=by_x), "mlp_x" if by_x else "mlp_y",
            [shape((PART, 2 * CH), BF)] * 4 + [shape((CELLS, HALF), BF)] * 2 + [shape((HALF, CH), BF)] * 2,
            normed, update, w_in[0].reshape(dims), w_out[0].reshape(dims), views={2: view, 3: view}, room=12,
        )
        return outs[:4], outs[4:]

    grads_b, kept_b = half(False)
    grads_b = around(grads_b, "y")
    grads_a, kept_a = half(True)
    a_one, a_three = send(grads_a[1], "x", 1), send(grads_a[3], "x", 3)
    d_hidden, d_one, d_two, a_two = run(
        finish_kernel, "finish",
        [shape((CELLS, CH), BF)] + [shape((48, CH), BF)] * 2 + [shape((PART, 2 * CH), BF)],
        kept_a[1], kept_b[1], kept_a[2], kept_b[2], norm_gain, hat, inv, grads_a[2], same={7: 3},
        scratch=[vm((CELLS, CH), F32)] + [vm((48, CH), F32)] * 2, room=12,
    )
    advanced, token = run(
        advance_kernel, "advance", [shape((CELLS, CH), BF), shape((8, LANES), F32)],
        kept_a[0], kept_b[0], kept_a[3], kept_b[3], state.reshape(CELLS, CH), keep, d_hidden,
        views={6: anywhere}, scratch=[vm((CELLS, CH), F32)], room=12,
    )
    grads_b = run(
        functools.partial(sum_four_kernel, by_x=False), "sum_y", [shape((64, 2 * CH), BF)] * 4,
        *grads_b, token, views={4: anywhere}, scratch=[vm((2, 2, 4, 16, 2 * CH), BF)],
    )
    d_one, d_two = swap_lon(d_one, d_two)
    grads_a = [grads_a[0], a_one, send(a_two, "x", 2), a_three]
    grads_b = around(grads_b, "x")
    grads_a = run(
        functools.partial(sum_four_kernel, by_x=True), "sum_x", [shape((64, 2 * CH), BF)] * 4,
        *grads_a, d_hidden, views={4: anywhere}, scratch=[vm((2, 4, 32, 2 * CH), BF)],
    )
    d_up, d_down = run(
        rim_pack_kernel, "rim_pack_back", [shape((176, CH), BF)] * 2, d_hidden, d_one, d_two, d_one,
        scratch=[vm((32, CH), F32)], views={3: anywhere},
    )
    d_above, d_below = swap_lat(d_up, d_down)
    grads_a = around(grads_a, "y")
    mine, other = run(
        sum_eight_kernel, "sum_xy", [shape((64, 2 * CH), BF)] * 2, *grads_a, *grads_b,
        scratch=[vm((4, 2, 16, 2 * CH), BF)],
    )
    other = send(other, "z_hi", 1)
    state_grad, token = run(
        conv_back_kernel, "conv_back", [shape((ROWS, COLS, CH), BF), shape((8, LANES), F32)],
        d_hidden, d_one, d_two, d_above, d_below, taps, upstream, mine, views={7: anywhere},
        scratch=[
            vm((BLOCKS, PAD_ROWS, PAD_COLS, LANES), F32), vm((BLOCKS, 49, 8, LANES), F32),
            vm((BLOCKS, ROWS, COLS, LANES), F32),
        ],
        room=10,
    )
    grads = run(
        sum_two_kernel, "sum_z_hi", [shape((16, 2 * CH), BF)] * 4, mine, other, token, views={2: anywhere},
        scratch=[vm((4, 16, 2 * CH), BF)],
    )
    grads = around(grads, "z_lo")
    grad_in, grad_out = run(sum_last_kernel, "sum_z", [shape((16, CH), F32)] * 2, *grads)
    return (
        advanced.reshape(1, ROWS, COLS, CH),
        state_grad[None],
        grad_in[None],
        grad_out[None],
    )


def solution(mesh):
    placed = (
        P("group", "lat", "lon", None),
        P("group", "lat", "lon", None),
        P("group", None, None, None),
        P("group", None),
        P("group", None, None),
        P("group", None, None),
        P("group", "lat", "lon", None),
        P("group", "lat", "lon", None),
        P("lat", "lon"),
    )
    return jax.shard_map(
        body,
        mesh=mesh,
        in_specs=placed,
        out_specs=(
            P("group", "lat", "lon", None),
            P("group", "lat", "lon", None),
            P("group", ("lat", "lon"), None),
            P("group", ("lat", "lon"), None),
        ),
        check_vma=False,
    )
```

```python
import functools

import jax
import jax.numpy as jnp
from jax import lax
from jax.experimental import pallas as pl
from jax.experimental.pallas import tpu as pltpu
from jax.sharding import PartitionSpec as P

Q = 8
EPS = 1e-06
BF = jnp.bfloat16
F32 = jnp.float32
ROWS, COLS, CH, LANES = 16, 48, 512, 128
CELLS = ROWS * COLS
BLOCKS = CH // LANES
RIM = 3
TAPS = 7
LEFT = 8
PAD_ROWS, PAD_COLS = ROWS + 2 * RIM, 64
HALF = 1024
PART = 256
GELU_A = 0.7978845608028654
GELU_B = 0.044715 * GELU_A


def shape(dims, dtype):
    return jax.ShapeDtypeStruct(dims, dtype)


def run(kernel, name, outs, *args, smem=0, scratch=(), views=None, room=4, same=None):
    views = views or {}
    in_specs = [
        pl.BlockSpec(memory_space=pltpu.SMEM)
        if at < smem
        else views.get(at, pl.BlockSpec(memory_space=pltpu.VMEM))
        for at in range(len(args))
    ]
    return pl.pallas_call(
        kernel,
        out_shape=outs,
        grid=(1,),
        in_specs=in_specs,
        out_specs=[pl.BlockSpec(memory_space=pltpu.VMEM)] * len(outs),
        scratch_shapes=list(scratch),
        input_output_aliases=same or {},
        compiler_params=pltpu.CompilerParams(vmem_limit_bytes=room << 20),
        cost_estimate=pl.CostEstimate(flops=0, bytes_accessed=1024, transcendentals=0),
        name=name,
    )(*args)


def lon_is_even():
    return lax.rem(lax.axis_index("lon"), 2) == 0


def cols_into(packed, row, cells, first):
    packed[3 * row : 3 * row + 3, :] = cells[first : first + 3, :]


def by_parity(even, a, b):
    return jnp.where(even, a, b)


def export_kernel(state_ref, out_ref, held, arrived):
    copy = pltpu.make_async_copy(state_ref.at[:, :, 0:LANES], held, arrived)
    copy.start()
    copy.wait()
    cells = held[...].reshape(CELLS, LANES).astype(F32)
    out_ref[...] = jnp.concatenate(
        [cells[at * LANES : (at + 1) * LANES].T[:Q] for at in range(CELLS // LANES)], axis=0
    ).astype(BF)


def lon_pack_kernel(state_ref, fields_ref, one_ref, two_ref, left, right):
    for row in range(ROWS):
        cols_into(left, row, state_ref[row, 0:16, LANES:].astype(F32), 0)
        cols_into(right, row, state_ref[row, 32:48, LANES:].astype(F32), 13)
    even = lon_is_even()
    one_ref[:, LANES:] = by_parity(even, right[...], left[...]).astype(BF)
    two_ref[:, LANES:] = by_parity(even, left[...], right[...]).astype(BF)
    one_ref[:, :LANES] = fields_ref[...]
    two_ref[:, :LANES] = fields_ref[...]


def sides(one_ref, two_ref):
    even = lon_is_even()
    one, two = one_ref[...].astype(F32), two_ref[...].astype(F32)
    return by_parity(even, two, one), by_parity(even, one, two)


def lat_pack_kernel(fields_ref, one_ref, two_ref, state_ref, up_ref, down_ref, hold):
    up_ref[80:224, :] = state_ref[0:RIM, :, LANES:].reshape(144, 384)
    down_ref[80:224, :] = state_ref[ROWS - RIM :, :, LANES:].reshape(144, 384)
    left, right = sides(one_ref, two_ref)
    hold[0:48, 0:128] = fields_ref[...].astype(F32)
    hold[0:48, 128:256] = left[:, :LANES]
    hold[0:48, 256:384] = right[:, :LANES]
    hold[64:80, :] = jnp.zeros((16, 384), F32)
    for out_ref, at in ((up_ref, 0), (down_ref, 39)):
        hold[48:57, :] = left[at : at + 9, LANES:]
        hold[57:66, :] = right[at : at + 9, LANES:]
        out_ref[0:80, :] = hold[...].astype(BF)


def import_kernel(
    source_ref, state_ref, weight_ref, fields_ref, one_ref, two_ref, above_ref, below_ref,
    forced_ref, send_one_ref, send_two_ref, tiles, cells, left, right, flat,
):
    lat, lon = lax.axis_index("lat"), lax.axis_index("lon")
    for row in range(ROWS):
        flat[0:4, row * COLS : (row + 1) * COLS] = weight_ref[row]
    places = []
    for pair in range(4):
        source = source_ref[pair]
        lat_step = source // 32 - lat + 1
        lon_step = lax.rem(lax.rem(source, 32) - lon + 33, 32)
        places.append(jnp.clip(lat_step * 3 + lon_step, 0, 8))
    lon_left, lon_right = sides(one_ref, two_ref)
    tiles[3] = lon_left[:, :LANES]
    tiles[4] = fields_ref[...].astype(F32)
    tiles[5] = lon_right[:, :LANES]
    for at, ref in ((0, above_ref), (6, below_ref)):
        tiles[at + 1] = ref[0:48, 0:128].astype(F32)
        tiles[at] = ref[0:48, 128:256].astype(F32)
        tiles[at + 2] = ref[0:48, 256:384].astype(F32)
    state = state_ref[:, :, 0:LANES].reshape(CELLS, LANES).astype(F32)
    for at in range(CELLS // LANES):
        running = jnp.zeros((Q, LANES), F32)
        for pair in range(4):
            weight = flat[pair : pair + 1, at * LANES : (at + 1) * LANES]
            running = running + weight * tiles[places[pair], at * Q : (at + 1) * Q, :]
        wide = jnp.concatenate(
            [jnp.zeros((Q, LANES), F32), running, jnp.zeros((LANES - 2 * Q, LANES), F32)], axis=0
        )
        cells[at * LANES : (at + 1) * LANES, :] = state[at * LANES : (at + 1) * LANES] + wide.T
    forced_ref[...] = cells[...].astype(BF)
    for row in range(ROWS):
        start = row * COLS
        left[3 * row : 3 * row + 3, :] = cells[start : start + 3, :]
        right[3 * row : 3 * row + 3, :] = cells[start + 45 : start + 48, :]
    even = lon_is_even()
    send_one_ref[...] = by_parity(even, right[...], left[...]).astype(BF)
    send_two_ref[...] = by_parity(even, left[...], right[...]).astype(BF)


def rim_pack_kernel(cells_ref, one_ref, two_ref, after_ref, up_ref, down_ref, hold):
    left, right = sides(one_ref, two_ref)
    width = hold.shape[1]
    hold[16:32, :] = jnp.zeros((16, width), F32)
    for out_ref, first, at in ((up_ref, 0, 0), (down_ref, CELLS - 144, 39)):
        out_ref[0:144, :] = cells_ref[first : first + 144, :]
        hold[0:9, :] = left[at : at + 9]
        hold[9:18, :] = right[at : at + 9]
        out_ref[144:176, :] = hold[...].astype(BF)


def spread_taps(spread, kernel_ref, lane_from, blocks, flipped):
    for at in range(blocks):
        for tap in range(TAPS * TAPS):
            from_tap = TAPS * TAPS - 1 - tap if flipped else tap
            spread[at, tap] = jnp.broadcast_to(kernel_ref[from_tap, lane_from + at : lane_from + at + 1, :], (8, LANES))


def fill_rows(pad, at, top, middle, bottom):
    pad[at, 0:RIM, LEFT : LEFT + COLS, :] = top
    pad[at, RIM : RIM + ROWS, LEFT : LEFT + COLS, :] = middle
    pad[at, RIM + ROWS :, LEFT : LEFT + COLS, :] = bottom


def fill_sides(pad, at, left, right, above, below):
    for row in range(PAD_ROWS):
        if row < RIM:
            one = above[3 * row : 3 * row + 3]
            two = above[9 + 3 * row : 12 + 3 * row]
        elif row < RIM + ROWS:
            one = left[3 * (row - RIM) : 3 * (row - RIM) + 3]
            two = right[3 * (row - RIM) : 3 * (row - RIM) + 3]
        else:
            low = row - RIM - ROWS
            one = below[3 * low : 3 * low + 3]
            two = below[9 + 3 * low : 12 + 3 * low]
        pad[at, row, LEFT - RIM : LEFT, :] = one
        pad[at, row, LEFT + COLS : LEFT + COLS + RIM, :] = two


PASSES = ((0, 1, 2), (3, 4), (5, 6))


def convolve(pad, spread, at, out):
    for first in (0, 24):
        cols = slice(first, first + 24)
        for shifts in PASSES:
            taps = {
                (off, shift): spread[at, off * TAPS + shift][None] for off in range(TAPS) for shift in shifts
            }
            sums = {}
            for row in range(PAD_ROWS):
                start = first + LEFT - RIM
                window = {
                    shift: pad[at, row, start + shift : start + shift + 24, :].reshape(3, 8, LANES)
                    for shift in shifts
                }
                for off in range(TAPS):
                    out_row = row - off
                    if 0 <= out_row < ROWS:
                        part = window[shifts[0]] * taps[off, shifts[0]]
                        for shift in shifts[1:]:
                            part = part + window[shift] * taps[off, shift]
                        if off > 0:
                            part = part + sums[out_row]
                        elif shifts[0] > 0:
                            part = part + out[at, out_row, cols, :].reshape(3, 8, LANES)
                        sums[out_row] = part
                if row >= TAPS - 1:
                    out_row = row - (TAPS - 1)
                    out[at, out_row, cols, :] = sums.pop(out_row).reshape(24, LANES)


def conv_wide_kernel(
    state_ref, one_ref, two_ref, above_ref, below_ref, kernel_ref, after_ref, hidden_ref, pad, spread, *, blocks
):
    left, right = sides(one_ref, two_ref)
    above = above_ref[48:80, :].astype(F32)
    below = below_ref[48:80, :].astype(F32)
    spread_taps(spread, kernel_ref, blocks[0] + 1, len(blocks), False)
    for at, block in enumerate(blocks):
        wide = slice((block + 1) * LANES, (block + 2) * LANES)
        thin = slice(block * LANES, (block + 1) * LANES)
        fill_rows(
            pad, at, above_ref[80:224, thin].astype(F32).reshape(RIM, COLS, LANES),
            state_ref[:, :, wide].astype(F32), below_ref[80:224, thin].astype(F32).reshape(RIM, COLS, LANES),
        )
        fill_sides(pad, at, left[:, wide], right[:, wide], above[:, thin], below[:, thin])

    def one_block(at, carry):
        convolve(pad, spread, at, hidden_ref)
        return carry

    lax.fori_loop(0, len(blocks), one_block, 0)


def masked_kernel(upstream_ref, mask_ref, after_ref, update_ref, keep_ref):
    mask = jnp.where(lax.axis_index("group") == 1, mask_ref[...].astype(F32), 1.0).T
    for row in range(ROWS):
        rows = slice(row * COLS, (row + 1) * COLS)
        keep_ref[rows, :] = jnp.broadcast_to(mask[:, row : row + 1], (COLS, LANES))
    for at in range(BLOCKS):
        lanes = slice(at * LANES, (at + 1) * LANES)
        update_ref[:, lanes] = (keep_ref[...] * upstream_ref[:, lanes].astype(F32)).astype(BF)


def conv_norm_kernel(
    forced_ref, one_ref, two_ref, above_ref, below_ref, kernel_ref, hidden_ref, more_ref, gain_ref,
    normed_ref, hat_ref, inv_ref, pad, spread, first,
):
    left, right = sides(one_ref, two_ref)
    above, below = above_ref[...].astype(F32), below_ref[...].astype(F32)
    spread_taps(spread, kernel_ref, 0, 1, False)
    fill_rows(
        pad, 0, above[0:144].reshape(RIM, COLS, LANES),
        forced_ref[...].astype(F32).reshape(ROWS, COLS, LANES), below[0:144].reshape(RIM, COLS, LANES),
    )
    fill_sides(pad, 0, left, right, above[144:176], below[144:176])

    convolve(pad, spread, 0, first)

    def one_row(row, carry):
        parts = [first[0, row], hidden_ref[0, row], more_ref[0, row], more_ref[1, row]]
        centre = jnp.sum(sum(parts[1:], parts[0]), axis=-1, keepdims=True) * (1.0 / CH)
        parts = [part - centre for part in parts]
        squares = [part * part for part in parts]
        variance = jnp.sum(sum(squares[1:], squares[0]), axis=-1, keepdims=True) * (1.0 / CH)
        inv = lax.rsqrt(variance + EPS)
        inv_ref[row] = jnp.broadcast_to(inv, (COLS, LANES))
        for at in range(BLOCKS):
            lanes = slice(at * LANES, (at + 1) * LANES)
            hat = parts[at] * inv
            hat_ref[row, :, lanes] = hat
            normed_ref[row, :, lanes] = (hat * gain_ref[:, lanes]).astype(BF)
        return carry

    lax.fori_loop(0, ROWS, one_row, 0, unroll=4)


def dot(a, b, left, right):
    return lax.dot_general(a, b, (((left,), (right,)), ((), ())), preferred_element_type=F32)


def along(axis):
    lon = lax.axis_index("lon")
    if axis == "x":
        return lax.rem(lon, 4)
    if axis == "y":
        return lon // 8
    return lax.rem(lon // 4, 2)


def mlp_kernel(
    normed_ref, update_ref, w_in_ref, w_out_ref,
    grad0_ref, grad1_ref, grad2_ref, grad3_ref, act_ref, pre_ref, w_in_out_ref, w_out_out_ref,
    *, by_x,
):
    def units(step):
        return slice(step * PART, (step + 1) * PART)

    for step in range(4):
        chunk = lax.rem(along("x" if by_x else "y") + step, 4)
        w_in_out_ref[units(step), :] = w_in_ref[0, :, chunk].reshape(PART, CH)
        w_out_out_ref[units(step), :] = w_out_ref[0, :, chunk].reshape(PART, CH)

    def expand(step, rows):
        value = dot(normed_ref[rows, :], w_in_out_ref[units(step), :], 1, 1)
        return value, dot(update_ref[rows, :], w_out_out_ref[units(step), :], 1, 1)

    def bend(step, rows, value, back):
        square = value * value
        bent = jnp.tanh(value * (GELU_A + GELU_B * square))
        cdf = 0.5 + 0.5 * bent
        act_ref[rows, units(step)] = (value * cdf).astype(BF)
        slope = cdf + (0.5 * value) * (1.0 - bent * bent) * (GELU_A + 3.0 * GELU_B * square)
        pre_ref[rows, units(step)] = (back * slope).astype(BF)

    grads = (grad0_ref, grad1_ref, grad2_ref, grad3_ref)
    pieces = [(step, slice(at, at + 256)) for step in range(4) for at in range(0, CELLS, 256)]
    held = expand(*pieces[0])
    for at, (step, rows) in enumerate(pieces):
        following = expand(*pieces[at + 1]) if at + 1 < len(pieces) else None
        bend(step, rows, *held)
        held = following
        if rows.stop == CELLS:
            grads[step][:, :CH] = dot(pre_ref[:, units(step)], normed_ref[...], 0, 0).astype(BF)
            grads[step][:, CH:] = dot(act_ref[:, units(step)], update_ref[...], 0, 0).astype(BF)


def advance_kernel(
    act_a_ref, act_b_ref, w_out_a_ref, w_out_b_ref, state_ref, keep_ref, after_ref, advanced_ref, token_ref, wide
):
    token_ref[...] = jnp.zeros((8, LANES), F32)
    wide[...] = dot(act_a_ref[...], w_out_a_ref[...], 1, 0) + dot(act_b_ref[...], w_out_b_ref[...], 1, 0)
    for at in range(BLOCKS):
        lanes = slice(at * LANES, (at + 1) * LANES)
        advanced_ref[:, lanes] = (state_ref[:, lanes].astype(F32) + keep_ref[...] * wide[:, lanes]).astype(BF)


def finish_kernel(
    pre_a_ref, pre_b_ref, w_in_a_ref, w_in_b_ref, gain_ref, hat_ref, inv_ref, passed_ref,
    d_hidden_ref, one_ref, two_ref, passed_out_ref, wide, left, right,
):
    wide[...] = dot(pre_a_ref[...], w_in_a_ref[...], 1, 0) + dot(pre_b_ref[...], w_in_b_ref[...], 1, 0)

    def one_row(row, carry):
        rows = pl.ds(pl.multiple_of(row * COLS, COLS), COLS)
        hat = hat_ref[rows, :]
        scaled = wide[rows, :] * gain_ref[...]
        plain = jnp.sum(scaled, axis=-1, keepdims=True) * (1.0 / CH)
        mixed = jnp.sum(scaled * hat, axis=-1, keepdims=True) * (1.0 / CH)
        back = inv_ref[rows, 0:1] * (scaled - plain - hat * mixed)
        wide[rows, :] = back
        d_hidden_ref[rows, :] = back.astype(BF)
        return carry

    lax.fori_loop(0, ROWS, one_row, 0, unroll=4)
    for row in range(ROWS):
        start = row * COLS
        left[3 * row : 3 * row + 3, :] = wide[start : start + 3, :]
        right[3 * row : 3 * row + 3, :] = wide[start + 45 : start + 48, :]
    even = lon_is_even()
    one_ref[...] = by_parity(even, right[...], left[...]).astype(BF)
    two_ref[...] = by_parity(even, left[...], right[...]).astype(BF)


def conv_back_kernel(
    d_hidden_ref, one_ref, two_ref, above_ref, below_ref, kernel_ref, upstream_ref, after_ref,
    out_ref, token_ref, pad, spread, held,
):
    left, right = sides(one_ref, two_ref)
    spread_taps(spread, kernel_ref, 0, BLOCKS, True)
    for at in range(BLOCKS):
        lanes = slice(at * LANES, (at + 1) * LANES)
        above, below = above_ref[:, lanes].astype(F32), below_ref[:, lanes].astype(F32)
        fill_rows(
            pad, at, above[0:144].reshape(RIM, COLS, LANES),
            d_hidden_ref[:, lanes].astype(F32).reshape(ROWS, COLS, LANES),
            below[0:144].reshape(RIM, COLS, LANES),
        )
        fill_sides(pad, at, left[:, lanes], right[:, lanes], above[144:176], below[144:176])

    token_ref[...] = jnp.zeros((8, LANES), F32)

    def one_block(at, carry):
        convolve(pad, spread, at, held)
        return carry

    lax.fori_loop(0, BLOCKS, one_block, 0)
    for at in range(BLOCKS):
        lanes = slice(at * LANES, (at + 1) * LANES)
        out_ref[:, :, lanes] = (upstream_ref[:, :, lanes].astype(F32) + held[at]).astype(BF)


def sum_refs(refs):
    total = refs[0][...].astype(F32)
    for ref in refs[1:]:
        total = total + ref[...].astype(F32)
    return total


def sum_four_kernel(a, b, c, d, after, out0, out1, out2, out3, hold, *, by_x):
    hold[...] = sum_refs((a, b, c, d)).astype(BF).reshape(hold.shape)
    for step, out in enumerate((out0, out1, out2, out3)):
        chunk = lax.rem(along("y" if by_x else "x") + step, 4)
        if by_x:
            out[...] = hold[:, chunk].reshape(out.shape)
        else:
            out[...] = hold[:, :, chunk].reshape(out.shape)


def sum_eight_kernel(*refs):
    ins, (mine, other), hold = refs[:8], refs[8:10], refs[10]
    hold[0:2] = sum_refs(ins[:4]).astype(BF).reshape(2, 2, 16, 2 * CH)
    hold[2:4] = sum_refs(ins[4:]).astype(BF).reshape(2, 2, 16, 2 * CH)
    at = along("z_hi")
    mine[...] = hold[:, at].reshape(64, 2 * CH)
    other[...] = hold[:, 1 - at].reshape(64, 2 * CH)


def sum_two_kernel(a, b, after, out0, out1, out2, out3, hold):
    hold[...] = sum_refs((a, b)).astype(BF).reshape(4, 16, 2 * CH)
    for step, out in enumerate((out0, out1, out2, out3)):
        out[...] = hold[lax.rem(lax.axis_index("lat") + step, 4)]


def sum_last_kernel(*refs):
    total = sum_refs(refs[:4])
    refs[4][...] = total[:, :CH]
    refs[5][...] = total[:, CH:]


def ring(axis):
    if axis == "x":
        lines = [[(i, a, b) for i in range(4)] for a in range(4) for b in range(8)]
    elif axis == "y":
        lines = [[(a, i, b) for i in range(4)] for a in range(4) for b in range(8)]
    elif axis == "z_hi":
        lines = [[(a, b, i + 4 * j) for j in range(2)] for a in range(4) for b in range(4) for i in range(4)]
    else:
        lines = [[(a, b, i + 4 * j) for i in range(4)] for a in range(4) for b in range(4) for j in range(2)]
    return [[(z % 4) * 32 + y * 8 + (z // 4) * 4 + x for x, y, z in line] for line in lines]


def send(piece, axis, step):
    groups = ring(axis)
    count = len(groups[0])
    pairs = [(g[i], g[(i + step) % count]) for g in groups for i in range(count)]
    return lax.ppermute(piece, ("lat", "lon"), pairs)


def around(pieces, axis):
    return [pieces[0]] + [send(piece, axis, step) for step, piece in enumerate(pieces) if step]


def swap_lon(one, two):
    pairs = [(i, i ^ 1) for i in range(32)]
    other = [(i, (i - 1) % 32 if i % 2 == 0 else (i + 1) % 32) for i in range(32)]
    two = lax.ppermute(two, "lon", other)
    return lax.ppermute(one, "lon", pairs), two


def swap_lat(up, down):
    above = lax.ppermute(down, "lat", [(i, i + 1) for i in range(3)])
    below = lax.ppermute(up, "lat", [(i + 1, i) for i in range(3)])
    return above, below


def body(
    states, cotangent, depth_kernel, norm_gain, w_in, w_out, source_tiles, regrid_weights, land_mask
):
    vm = pltpu.VMEM
    state = states[0]
    upstream = cotangent[0]
    taps = depth_kernel[0].reshape(TAPS * TAPS, BLOCKS, LANES)
    sources = source_tiles.reshape(4)
    weights = regrid_weights[0].transpose(0, 2, 1)

    (mine,) = run(
        export_kernel, "export", [shape((48, LANES), BF)], state, views={0: pl.BlockSpec(memory_space=pl.ANY)},
        scratch=[vm((ROWS, COLS, LANES), BF), pltpu.SemaphoreType.DMA], room=60,
    )
    fields = lax.ppermute(mine, "group", [(0, 1), (1, 0)])
    one, two = run(
        lon_pack_kernel, "lon_pack", [shape((48, CH), BF)] * 2, state, fields,
        scratch=[vm((48, 384), F32)] * 2,
    )
    one, two = swap_lon(one, two)
    up, down = run(
        lat_pack_kernel, "lat_pack", [shape((224, 384), BF)] * 2, fields, one, two, state,
        scratch=[vm((80, 384), F32)],
    )
    above, below = swap_lat(up, down)
    anywhere = pl.BlockSpec(memory_space=pl.ANY)
    forced, f_one, f_two = run(
        import_kernel, "import", [shape((CELLS, LANES), BF)] + [shape((48, LANES), BF)] * 2,
        sources, state, weights, fields, one, two, above, below, smem=1,
        scratch=[vm((9, 48, LANES), F32), vm((CELLS, LANES), F32)] + [vm((48, LANES), F32)] * 2
        + [vm((8, CELLS), F32)],
    )
    f_one, f_two = swap_lon(f_one, f_two)
    update, keep = run(
        masked_kernel, "masked", [shape((CELLS, CH), BF), shape((CELLS, LANES), F32)],
        upstream.reshape(CELLS, CH), land_mask, forced, views={2: anywhere},
    )
    (hidden,) = run(
        functools.partial(conv_wide_kernel, blocks=(0,)), "conv_one", [shape((1, ROWS, COLS, LANES), F32)],
        state, one, two, above, below, taps, keep, views={6: anywhere},
        scratch=[vm((1, PAD_ROWS, PAD_COLS, LANES), F32), vm((1, 49, 8, LANES), F32)], room=6,
    )
    f_up, f_down = run(
        rim_pack_kernel, "rim_pack", [shape((176, LANES), BF)] * 2, forced, f_one, f_two, hidden,
        scratch=[vm((32, LANES), F32)], views={3: pl.BlockSpec(memory_space=pl.ANY)},
    )
    f_above, f_below = swap_lat(f_up, f_down)
    (more,) = run(
        functools.partial(conv_wide_kernel, blocks=(1, 2)), "conv_two", [shape((2, ROWS, COLS, LANES), F32)],
        state, one, two, above, below, taps, f_up, views={6: anywhere},
        scratch=[vm((2, PAD_ROWS, PAD_COLS, LANES), F32), vm((2, 49, 8, LANES), F32)], room=6,
    )
    normed, hat, inv = run(
        conv_norm_kernel, "conv_norm",
        [shape((ROWS, COLS, CH), BF), shape((ROWS, COLS, CH), F32), shape((ROWS, COLS, LANES), F32)],
        forced, f_one, f_two, f_above, f_below, taps, hidden, more, norm_gain,
        scratch=[vm((1, PAD_ROWS, PAD_COLS, LANES), F32), vm((1, 49, 8, LANES), F32), vm((1, ROWS, COLS, LANES), F32)],
        room=6,
    )
    normed = normed.reshape(CELLS, CH)
    hat = hat.reshape(CELLS, CH)
    inv = inv.reshape(CELLS, LANES)

    def half(by_x):
        if by_x:
            dims, block, at = (2, 16, 4, 16, CH), (1, 16, 4, 16, CH), lambda i: (0, 0, 0, 0, 0)
        else:
            dims, block, at = (2, 2, 4, 128, CH), (1, 2, 4, 128, CH), lambda i: (1, 0, 0, 0, 0)
        view = pl.BlockSpec(block, at)
        outs = run(
            functools.partial(mlp_kernel, by_x=by_x), "mlp_x" if by_x else "mlp_y",
            [shape((PART, 2 * CH), BF)] * 4 + [shape((CELLS, HALF), BF)] * 2 + [shape((HALF, CH), BF)] * 2,
            normed, update, w_in[0].reshape(dims), w_out[0].reshape(dims), views={2: view, 3: view}, room=12,
        )
        return outs[:4], outs[4:]

    grads_b, kept_b = half(False)
    grads_b = around(grads_b, "y")
    grads_a, kept_a = half(True)
    a_one, a_three = send(grads_a[1], "x", 1), send(grads_a[3], "x", 3)
    d_hidden, d_one, d_two, a_two = run(
        finish_kernel, "finish",
        [shape((CELLS, CH), BF)] + [shape((48, CH), BF)] * 2 + [shape((PART, 2 * CH), BF)],
        kept_a[1], kept_b[1], kept_a[2], kept_b[2], norm_gain, hat, inv, grads_a[2], same={7: 3},
        scratch=[vm((CELLS, CH), F32)] + [vm((48, CH), F32)] * 2, room=12,
    )
    advanced, token = run(
        advance_kernel, "advance", [shape((CELLS, CH), BF), shape((8, LANES), F32)],
        kept_a[0], kept_b[0], kept_a[3], kept_b[3], state.reshape(CELLS, CH), keep, d_hidden,
        views={6: anywhere}, scratch=[vm((CELLS, CH), F32)], room=12,
    )
    grads_b = run(
        functools.partial(sum_four_kernel, by_x=False), "sum_y", [shape((64, 2 * CH), BF)] * 4,
        *grads_b, token, views={4: anywhere}, scratch=[vm((2, 2, 4, 16, 2 * CH), BF)],
    )
    d_one, d_two = swap_lon(d_one, d_two)
    grads_a = [grads_a[0], a_one, send(a_two, "x", 2), a_three]
    grads_b = around(grads_b, "x")
    grads_a = run(
        functools.partial(sum_four_kernel, by_x=True), "sum_x", [shape((64, 2 * CH), BF)] * 4,
        *grads_a, d_hidden, views={4: anywhere}, scratch=[vm((2, 4, 32, 2 * CH), BF)],
    )
    d_up, d_down = run(
        rim_pack_kernel, "rim_pack_back", [shape((176, CH), BF)] * 2, d_hidden, d_one, d_two, d_one,
        scratch=[vm((32, CH), F32)], views={3: anywhere},
    )
    d_above, d_below = swap_lat(d_up, d_down)
    grads_a = around(grads_a, "y")
    mine, other = run(
        sum_eight_kernel, "sum_xy", [shape((64, 2 * CH), BF)] * 2, *grads_a, *grads_b,
        scratch=[vm((4, 2, 16, 2 * CH), BF)],
    )
    other = send(other, "z_hi", 1)
    state_grad, token = run(
        conv_back_kernel, "conv_back", [shape((ROWS, COLS, CH), BF), shape((8, LANES), F32)],
        d_hidden, d_one, d_two, d_above, d_below, taps, upstream, mine, views={7: anywhere},
        scratch=[
            vm((BLOCKS, PAD_ROWS, PAD_COLS, LANES), F32), vm((BLOCKS, 49, 8, LANES), F32),
            vm((BLOCKS, ROWS, COLS, LANES), F32),
        ],
        room=10,
    )
    grads = run(
        sum_two_kernel, "sum_z_hi", [shape((16, 2 * CH), BF)] * 4, mine, other, token, views={2: anywhere},
        scratch=[vm((4, 16, 2 * CH), BF)],
    )
    grads = around(grads, "z_lo")
    grad_in, grad_out = run(sum_last_kernel, "sum_z", [shape((16, CH), F32)] * 2, *grads)
    return (
        advanced.reshape(1, ROWS, COLS, CH),
        state_grad[None],
        grad_in[None],
        grad_out[None],
    )


def solution(mesh):
    placed = (
        P("group", "lat", "lon", None),
        P("group", "lat", "lon", None),
        P("group", None, None, None),
        P("group", None),
        P("group", None, None),
        P("group", None, None),
        P("group", "lat", "lon", None),
        P("group", "lat", "lon", None),
        P("lat", "lon"),
    )
    return jax.shard_map(
        body,
        mesh=mesh,
        in_specs=placed,
        out_specs=(
            P("group", "lat", "lon", None),
            P("group", "lat", "lon", None),
            P("group", ("lat", "lon"), None),
            P("group", ("lat", "lon"), None),
        ),
        check_vma=False,
    )
```
